128 devices in a mesh: dp: 2 (over core), expert: 64 (over z, y, x).
Axes of the slice: x: 4, y: 4, z: 4, core: 2. Of those that a mesh axis runs over, the one named last changes fastest.
Arguments:
- tokens: bfloat16 [1536, 5120], P(('dp', 'expert')), may hold values from -6 to 6
- router_weight: bfloat16 [1536], P(('dp', 'expert')), may hold values from 0.19921875 to 1
- initial_id: int32 [1536, 1], P(('dp', 'expert')), may hold values from 0 to 3; in each aligned block of 768 rows (0 to 767, 768 to 1535, ...) at most 320 rows name the same one
- group_map: int32 [4], replicated, may hold values from 0 to 1, as said below
- teacher_gate: bfloat16 [5120, 16384], P(None, 'expert'), may hold values from -0.078125 to 0.078125
- teacher_up: bfloat16 [5120, 16384], P(None, 'expert'), may hold values from -0.078125 to 0.078125
- teacher_down: bfloat16 [16384, 5120], P('expert'), may hold values from -0.09375 to 0.09375
- student_gate: bfloat16 [5120, 8192], P(None, 'expert'), may hold values from -0.078125 to 0.078125
- student_up: bfloat16 [5120, 8192], P(None, 'expert'), may hold values from -0.078125 to 0.078125
- student_down: bfloat16 [8192, 5120], P('expert'), may hold values from -0.09375 to 0.09375
Outputs:
- grad_gate: float32 [5120, 8192], P('dp', 'expert')
- grad_up: float32 [5120, 8192], P('dp', 'expert')
- grad_down: float32 [8192, 5120], P('expert', 'dp')
The draws below stay inside these ranges and needn't reach their ends.
Inputs may be any that keep to these rules, and one draw needn't show every extreme that they name: `initial_id`: in each half of the tokens (rows h * 12 * 64 to (h + 1) * 12 * 64 - 1, h = 0, 1) every initial expert is named by at most 320 tokens, and some expert of some half by exactly 320. `group_map`: every merged expert is named by exactly 2 entries.
All inputs are finite; a program needn't handle non-finite values.
Results may differ from the reference program's by a relative error of at most 0.013.
Values may be sent and summed in bfloat16 or wider, within the bound.
No kernel may reach another device: no remote copies, remote signals or barrier semaphores. Data moves between devices by JAX's collectives and lax.ppermute only.
A program may use at most 128 MiB of HBM per device.

```python
import math
import jax
import jax.numpy as jnp
import numpy as np

D = 5120
F = 4096
E_ORIG = 4
GROUP = 2
E_MERGE = 2
TOK_DEV = 12
TOKENS = 1536
CAP = 320
N_EXPERT = 64


def draw_group_map(key, part):
    key = jax.random.fold_in(key, 7)
    return (jax.random.permutation(key, E_ORIG) // GROUP).astype(jnp.int32)


def steps_of(own_key, shape, cuts, least, top_value):
    loudness, own = 1.0, jax.random.fold_in(own_key, 6)
    for axis_at, blocks in cuts:
        heights = jnp.exp(jax.random.uniform(jax.random.fold_in(own, axis_at), (blocks,), jnp.float32, least / len(cuts), top_value / len(cuts)))
        loudness = loudness * jnp.repeat(heights, shape[axis_at] // blocks).reshape([-1 if axis == axis_at else 1 for axis in range(len(shape))])
    return loudness


def routed_block(stream_key, own, number, rows, amount, top, bound, lean):
    sequence = jax.random.permutation(stream_key, amount)
    packed, common = portions_of(amount, rows * top, bound, lean, True), portions_of(amount, rows * top, bound, lean, False)
    places = jnp.arange(amount)

    def named(sizes, rotation):
        used = int((sizes > 0).sum())
        fixed = max(1, used // 4)
        shifted = fixed + (places - fixed + rotation * (used - fixed)) % max(1, amount - fixed)
        return jnp.zeros((amount,), jnp.int32).at[sequence[jnp.where(places < fixed, places, shifted)]].set(jnp.asarray(sizes, jnp.int32))

    sizes = jnp.where(number % 4 == 0, named(packed, number // 4), named(common, number - number // 4 - 1))
    mixed = jax.random.permutation(jax.random.fold_in(own, 3), amount)
    giver, sink = mixed[0:amount // 2 * 2:2], mixed[1:amount // 2 * 2:2]
    slack = jnp.minimum(sizes[giver] - 1, bound - sizes[sink]) // 2
    slack = jnp.where((giver == sequence[0]) | (sink == sequence[0]) | (sizes[sink] == 0), 0, jnp.maximum(slack, 0))
    shifted = jax.random.randint(jax.random.fold_in(own, 4), (amount // 2,), 0, 1 << 20) % (slack + 1)
    sizes = sizes.at[giver].add(-shifted).at[sink].add(shifted)
    members = jnp.searchsorted(jnp.cumsum(sizes), jnp.arange(rows * top), side="right").astype(jnp.int32)
    grid = members.reshape(top, rows).T
    grid = grid[jax.random.permutation(jax.random.fold_in(own, 1), rows)]
    rotation = jax.random.randint(jax.random.fold_in(own, 2), (rows, 1), 0, top)
    return jnp.take_along_axis(grid, (jnp.arange(top)[None, :] + rotation) % top, axis=1)


def portions_of(amount, total, bound, slope, full):
    portions = [(1 << 20) // math.isqrt(standing ** slope) + 1 for standing in range(1, amount + 1)]
    largest = bound if full else min(bound, max(-(-total // amount), total * portions[0] // sum(portions)))
    least = 1 if total - largest >= amount - 1 else 0
    counts, rest = [largest] + [least] * (amount - 1), total - largest - least * (amount - 1)
    while rest > 0:
        movable = [i for i in range(1, amount) if counts[i] < largest] or [i for i in range(1, amount) if counts[i] < bound]
        whole, left = sum([portions[i] for i in movable]), rest
        for i in movable:
            extra = min(bound - counts[i], max(1, left * portions[i] // whole), rest)
            counts[i] = counts[i] + extra
            rest = rest - extra
    return np.array(counts)


def noise(key, shape, deviation, reach, shards=(), kind=jnp.bfloat16):
    factor_of = steps_of(key, shape, shards, -0.22, 0.18) if shards else 1.0
    result = jax.random.normal(key, shape, jnp.float32) * deviation * factor_of
    return jnp.minimum(jnp.maximum(result, -reach), reach).astype(kind)


def setup_inputs(seed: int = 0) -> dict:
    arg_keys = jax.random.split(jax.random.key(seed), 11)
    tokens = noise(arg_keys[0], (TOKENS, D), 1.0, 6.0, ((0, 128),))
    router_weight = jnp.clip(0.19921875 + 0.80078125 * jax.random.uniform(arg_keys[1], (TOKENS,), jnp.float32) ** steps_of(arg_keys[1], (TOKENS,), ((0, 128),), -0.2, 0.2), 0.19921875, 1.0).astype(jnp.bfloat16)
    initial_id_keys = jax.random.split(jax.random.fold_in(arg_keys[2], 1), TOKENS // (TOK_DEV * N_EXPERT))
    initial_id_turns = jax.random.permutation(jax.random.fold_in(arg_keys[2], 3), TOKENS // (TOK_DEV * N_EXPERT))
    initial_id = jax.vmap(lambda own, number: routed_block(jax.random.fold_in(arg_keys[2], 2), own, number, TOK_DEV * N_EXPERT, E_ORIG, 1, CAP, 1))(initial_id_keys, initial_id_turns).reshape((TOKENS, 1))
    group_map = draw_group_map(jax.random.fold_in(arg_keys[10], 71), 0)
    teacher_gate = noise(arg_keys[4], (D, E_ORIG * F), D ** -0.5, 0.078125, ((1, 64),))
    teacher_up = noise(arg_keys[5], (D, E_ORIG * F), D ** -0.5, 0.078125, ((1, 64),))
    teacher_down = noise(arg_keys[6], (E_ORIG * F, D), F ** -0.5, 0.09375, ((0, 64),))
    student_gate = noise(arg_keys[7], (D, E_MERGE * F), D ** -0.5, 0.078125, ((1, 64),))
    student_up = noise(arg_keys[8], (D, E_MERGE * F), D ** -0.5, 0.078125, ((1, 64),))
    student_down = noise(arg_keys[9], (E_MERGE * F, D), F ** -0.5, 0.09375, ((0, 64),))
    return dict(tokens=tokens, router_weight=router_weight, initial_id=initial_id, group_map=group_map, teacher_gate=teacher_gate, teacher_up=teacher_up, teacher_down=teacher_down, student_gate=student_gate, student_up=student_up, student_down=student_down)


def expert_forward(rows, w_gate, w_up):
    gate = jnp.dot(rows, w_gate, preferred_element_type=jnp.float32)
    upper = jnp.dot(rows, w_up, preferred_element_type=jnp.float32)
    hidden = (jax.nn.silu(gate) * upper).astype(jnp.bfloat16)
    return (gate, upper, hidden)

def reference(tokens, router_weight, initial_id, group_map, teacher_gate, teacher_up, teacher_down, student_gate, student_up, student_down):
    ids = initial_id[:, 0]
    weight = router_weight.astype(jnp.float32)
    teacher = jnp.zeros((TOKENS, D), jnp.float32)
    for orig in range(E_ORIG):
        cols = slice(orig * F, (orig + 1) * F)
        gate, upper, hidden = expert_forward(tokens, teacher_gate[:, cols], teacher_up[:, cols])
        out_rows = jnp.dot(hidden, teacher_down[cols, :], preferred_element_type=jnp.float32)
        teacher = jnp.where((ids == orig)[:, None], out_rows, teacher)
    merged_of = group_map[ids]
    student = jnp.zeros((TOKENS, D), jnp.float32)
    saved = []
    for merged in range(E_MERGE):
        cols = slice(merged * F, (merged + 1) * F)
        gate, upper, hidden = expert_forward(tokens, student_gate[:, cols], student_up[:, cols])
        out_rows = jnp.dot(hidden, student_down[cols, :], preferred_element_type=jnp.float32)
        student = jnp.where((merged_of == merged)[:, None], out_rows, student)
        saved.append((gate, upper, hidden))
    mismatch = weight[:, None] * (student - teacher)
    cotangent = (weight[:, None] * mismatch / math.sqrt(TOKENS)).astype(jnp.bfloat16)
    gate_parts, up_parts, down_parts = ([], [], [])
    for merged in range(E_MERGE):
        cols = slice(merged * F, (merged + 1) * F)
        gate, upper, hidden = saved[merged]
        chosen = jnp.where((merged_of == merged)[:, None], cotangent, jnp.zeros_like(cotangent))
        dhidden = jnp.dot(chosen, student_down[cols, :].T, preferred_element_type=jnp.float32)
        sigma = jax.nn.sigmoid(gate)
        dgate = (dhidden * upper * sigma * (1.0 + gate * (1.0 - sigma))).astype(jnp.bfloat16)
        dup = (dhidden * jax.nn.silu(gate)).astype(jnp.bfloat16)
        gate_parts.append(jnp.dot(tokens.T, dgate, preferred_element_type=jnp.float32))
        up_parts.append(jnp.dot(tokens.T, dup, preferred_element_type=jnp.float32))
        down_parts.append(jnp.dot(hidden.T, chosen, preferred_element_type=jnp.float32))
    return (jnp.concatenate(gate_parts, axis=1), jnp.concatenate(up_parts, axis=1), jnp.concatenate(down_parts, axis=0))
```

```python
import functools
import math

import jax
import jax.numpy as jnp
from jax import lax
from jax.experimental import pallas as pl
from jax.experimental.pallas import tpu as pltpu
from jax.sharding import PartitionSpec as P

F = 4096
E_ORIG = 4
META = 128
BF = jnp.bfloat16
F32 = jnp.float32
AXES = ("dp", "expert")
SIDE = 4


def coords(device):
    return device // 64, {"z": (device // 16) % SIDE, "y": (device // 4) % SIDE, "x": device % SIDE}


def number(core, at):
    return core * 64 + at["z"] * 16 + at["y"] * 4 + at["x"]


def swap_pairs(links):
    pairs = []
    for device in range(128):
        core, at = coords(device)
        axis, bits = links[core]
        pairs.append((device, number(core, {**at, axis: at[axis] ^ bits})))
    return pairs


def shift_pairs(axes, by):
    pairs = []
    for device in range(128):
        core, at = coords(device)
        axis = axes[core]
        pairs.append((device, number(core, {**at, axis: (at[axis] + by) % SIDE})))
    return pairs


def swap(value, links):
    return lax.ppermute(value, AXES, swap_pairs(links))


def shift(value, axes, by):
    return lax.ppermute(value, AXES, shift_pairs(axes, by))


FIRST = ("x", "z")
A3, A4 = (("y", 1), ("y", 3)), (("y", 3), ("y", 1))
B3, B4 = (("z", 1), ("x", 1)), (("z", 3), ("x", 3))
STEP5 = ((("z", 1), ("x", 1)), (("z", 3), ("x", 3)), (("y", 1), ("y", 3)))
STEP6 = ((("z", 3), ("x", 3)), (("z", 1), ("x", 1)), (("y", 3), ("y", 1)))


def join(*parts):
    return jnp.concatenate(parts, axis=0)


def grow(a32, b16):
    a64 = join(a32, swap(a32, A3))
    b32 = join(b16, swap(b16, B3))
    a64_far = swap(a64, A4)
    b64 = join(b32, swap(b32, B4))
    near = [join(v, swap(v, link)) for v, link in zip((a64, a64_far, b64), STEP5)]
    far = [swap(v, link) for v, link in zip(near, STEP6)]
    return near, far


def shrink(near, far):
    add = lambda mine, got: mine.astype(F32) + got.astype(F32)
    got = [swap(v, link) for v, link in zip(far, STEP6)]
    got = [(add(m[64:], g[64:]).astype(BF), add(m[:64], g[:64])) for m, g in zip(near, got)]
    a1, a2, b = [add(mine, swap(theirs, link)) for (theirs, mine), link in zip(got, STEP5)]
    a = add(a1, swap(a2.astype(BF), A4))
    b = add(b[:32], swap(b[32:].astype(BF), B4))
    a = add(a[:32], swap(a[32:].astype(BF), A3))
    b = add(b[:16], swap(b[16:].astype(BF), B3))
    return join(a, b)


def line_up_kernel(place_ref, own, one, two, three, a_ref, b_ref):
    place = place_ref[0]
    row = lax.broadcasted_iota(jnp.int32, (48, 64), 0)
    column = lax.broadcasted_iota(jnp.int32, (48, 64), 1)
    block, token = column // 16, column % 16
    source = (place + SIDE - block) % SIDE
    pick = jnp.where((row == source * 12 + token) & (token < 12), 1.0, 0.0).astype(BF)
    rows = jnp.concatenate([own[...], one[...], two[...], three[...]], axis=0)
    out = jnp.dot(pick, rows, preferred_element_type=F32).astype(BF)
    a_ref[...] = out[:32]
    b_ref[...] = out[32:]


def line_up(place, blocks):
    width = blocks[0].shape[1]
    vmem = pl.BlockSpec(memory_space=pltpu.VMEM)
    return pl.pallas_call(
        line_up_kernel,
        out_shape=[jax.ShapeDtypeStruct((32, width), BF), jax.ShapeDtypeStruct((16, width), BF)],
        in_specs=[pl.BlockSpec(memory_space=pltpu.SMEM)] + [vmem] * 4,
        out_specs=[vmem, vmem],
        compiler_params=pltpu.CompilerParams(vmem_limit_bytes=32 << 20),
    )(place, *blocks)


def forward_kernel(count, steps, info, *refs):
    xs, metas = refs[:count], refs[count : 2 * count]
    tg, tu, sg, su, h_ref, ab_ref, acc = refs[2 * count :]
    step = pl.program_id(0)
    x = jnp.concatenate([r[...] for r in xs], axis=0)
    w = jnp.concatenate([tg[...], tu[...], sg[...], su[...]], axis=1)
    part = jnp.dot(x, w, preferred_element_type=F32)

    @pl.when(step == 0)
    def _():
        acc[...] = part

    @pl.when(step > 0)
    def _():
        acc[...] += part

    @pl.when(step == steps - 1)
    def _():
        ids = jnp.concatenate([r[:, 1:2] for r in metas], axis=0).astype(F32)
        mask_t = ids == info[0].astype(F32)
        mask_s = jnp.zeros(ids.shape, F32)
        for i in range(E_ORIG):
            mask_s = mask_s + jnp.where(ids == float(i), info[1 + i].astype(F32), 0.0)
        mask_s = mask_s > 0.5
        gate, up = acc[:, 0:256], acc[:, 256:512]
        hid_t = gate * jax.nn.sigmoid(gate) * up
        h_ref[:, 128:384] = jnp.where(mask_t, -hid_t, 0.0).astype(BF)
        gate, up = acc[:, 512:640], acc[:, 640:768]
        sig = jax.nn.sigmoid(gate)
        silu = gate * sig
        h_ref[:, 0:128] = jnp.where(mask_s, silu * up, 0.0).astype(BF)
        ab_ref[:, 0:128] = jnp.where(mask_s, up * sig * (1.0 + gate * (1.0 - sig)), 0.0)
        ab_ref[:, 128:256] = jnp.where(mask_s, silu, 0.0)


def forward(info, chunks, tg, tu, sg, su):
    count, depth = len(chunks), tg.shape[0]
    rows, block = 128 * count, 512
    steps = depth // block
    at_k = lambda k: (k, 0)
    return pl.pallas_call(
        functools.partial(forward_kernel, count, steps),
        grid=(steps,),
        out_shape=[jax.ShapeDtypeStruct((rows, 384), BF), jax.ShapeDtypeStruct((rows, 256), F32)],
        in_specs=[pl.BlockSpec(memory_space=pltpu.SMEM)]
        + [pl.BlockSpec((128, block), lambda k: (0, k))] * count
        + [pl.BlockSpec((128, META), lambda k: (0, depth // META))] * count
        + [pl.BlockSpec((block, w.shape[1]), at_k) for w in (tg, tu, sg, su)],
        out_specs=[pl.BlockSpec((rows, 384), lambda k: (0, 0)), pl.BlockSpec((rows, 256), lambda k: (0, 0))],
        scratch_shapes=[pltpu.VMEM((rows, 768), F32)],
        compiler_params=pltpu.CompilerParams(vmem_limit_bytes=40 << 20),
        cost_estimate=pl.CostEstimate(flops=2 * rows * depth * 768, bytes_accessed=2 * depth * (rows + 768), transcendentals=0),
    )(info, *chunks, *chunks, tg, tu, sg, su)


def down_kernel(count, h_ref, sd, td, *outs):
    w = jnp.concatenate([sd[...], td[...]], axis=0)
    out = jnp.dot(h_ref[...], w, preferred_element_type=F32).astype(BF)
    for i in range(count):
        outs[i][...] = out[128 * i : 128 * (i + 1)]


def down(hidden, sd, td):
    rows, width = hidden.shape[0], sd.shape[1]
    count, block = rows // 128, 1280
    return pl.pallas_call(
        functools.partial(down_kernel, count),
        grid=(width // block,),
        out_shape=[jax.ShapeDtypeStruct((128, width), BF)] * count,
        in_specs=[
            pl.BlockSpec((rows, 384), lambda n: (0, 0)),
            pl.BlockSpec((128, block), lambda n: (0, n)),
            pl.BlockSpec((256, block), lambda n: (0, n)),
        ],
        out_specs=[pl.BlockSpec((128, block), lambda n: (0, n))] * count,
        compiler_params=pltpu.CompilerParams(vmem_limit_bytes=40 << 20),
        cost_estimate=pl.CostEstimate(flops=2 * rows * width * 384, bytes_accessed=2 * width * (rows + 384), transcendentals=0),
    )(hidden, sd, td)


def backward_kernel(count, half, core, *refs):
    xs, cs = refs[:count], refs[count : 2 * count]
    sd, h1, h2, ab1, ab2, send, keep, acc, gt, ht = refs[2 * count :]
    step = pl.program_id(0)
    c = jnp.concatenate([r[...] for r in cs], axis=0)

    @pl.when(step < 2 * half)
    def _():
        part = lax.dot_general(c, sd[...], (((1,), (1,)), ((), ())), preferred_element_type=F32)

        @pl.when(step == 0)
        def _():
            acc[...] = part

        @pl.when(step > 0)
        def _():
            acc[...] += part

    @pl.when(step == 2 * half - 1)
    def _():
        ab = jnp.concatenate([ab1[...], ab2[...]], axis=0)
        gt[0:128, :] = (acc[...] * ab[:, 0:128]).T.astype(BF)
        gt[128:256, :] = (acc[...] * ab[:, 128:256]).T.astype(BF)
        ht[...] = jnp.concatenate([h1[...], h2[...]], axis=0).astype(F32).T.astype(BF)

    @pl.when(step >= 2 * half)
    def _():
        x = jnp.concatenate([r[...] for r in xs], axis=0)
        out = jnp.concatenate(
            [jnp.dot(gt[...], x, preferred_element_type=F32), jnp.dot(ht[...], c, preferred_element_type=F32)],
            axis=0,
        )

        @pl.when(step < 3 * half)
        def _():
            send[...] = out.astype(BF)

        @pl.when(step >= 3 * half)
        def _():
            keep[...] = out


def backward(core, xs, cs, sd, h1, h2, ab1, ab2):
    count, width = len(xs), sd.shape[1]
    rows, block = 128 * count, 1280
    half = width // block // 2
    turn = lambda s, core: lax.rem(s + (1 - core[0]) * half, 2 * half)
    x_at = lambda s, core: (0, turn(jnp.maximum(s, 2 * half), core))
    c_at = lambda s, core: (0, turn(s, core))
    d_at = lambda s, core: (0, turn(jnp.minimum(s, 2 * half - 1), core))
    whole = lambda s, core: (0, 0)
    return pl.pallas_call(
        functools.partial(backward_kernel, count, half),
        grid_spec=pltpu.PrefetchScalarGridSpec(
            num_scalar_prefetch=1,
            grid=(4 * half,),
            in_specs=[pl.BlockSpec((128, block), x_at)] * count
            + [pl.BlockSpec((128, block), c_at)] * count
            + [pl.BlockSpec((128, block), d_at)]
            + [pl.BlockSpec((rows // 2, 128), whole)] * 2
            + [pl.BlockSpec((rows // 2, 256), whole)] * 2,
            out_specs=[
                pl.BlockSpec((384, block), lambda s, core: (0, jnp.clip(s - 2 * half, 0, half - 1))),
                pl.BlockSpec((384, block), lambda s, core: (0, jnp.maximum(s - 3 * half, 0))),
            ],
            scratch_shapes=[pltpu.VMEM((rows, 128), F32), pltpu.VMEM((256, rows), BF), pltpu.VMEM((128, rows), BF)],
        ),
        out_shape=[jax.ShapeDtypeStruct((384, width // 2), BF), jax.ShapeDtypeStruct((384, width // 2), F32)],
        compiler_params=pltpu.CompilerParams(vmem_limit_bytes=48 << 20),
        cost_estimate=pl.CostEstimate(flops=2 * rows * width * 512, bytes_accessed=6 * rows * width, transcendentals=0),
    )(core, *xs, *cs, sd, h1, h2, ab1, ab2)


def finish_kernel(keep, got, gate, up, low):
    out = keep[...] + got[...].astype(F32)
    gate[...] = out[0:128].T
    up[...] = out[128:256].T
    low[...] = out[256:384]


def finish(keep, got):
    width, block = keep.shape[1], 512
    wide = pl.BlockSpec((384, block), lambda n: (0, n))
    tall = pl.BlockSpec((block, 128), lambda n: (n, 0))
    return pl.pallas_call(
        finish_kernel,
        grid=(width // block,),
        out_shape=[jax.ShapeDtypeStruct((width, 128), F32)] * 2 + [jax.ShapeDtypeStruct((128, width), F32)],
        in_specs=[wide, wide],
        out_specs=[tall, tall, pl.BlockSpec((128, block), lambda n: (0, n))],
        compiler_params=pltpu.CompilerParams(vmem_limit_bytes=32 << 20),
    )(keep, got)


def per_device(
    tokens,
    router_weight,
    initial_id,
    group_map,
    teacher_gate,
    teacher_up,
    teacher_down,
    student_gate,
    student_up,
    student_down,
):
    core, owner = lax.axis_index("dp"), lax.axis_index("expert")
    total = tokens.shape[0] * 128
    place = jnp.where(core == 0, owner % SIDE, owner // 16).astype(jnp.int32).reshape(1)
    teacher_expert = owner * teacher_gate.shape[1] // F
    student_expert = owner * student_gate.shape[1] // F
    info = jnp.concatenate([teacher_expert.astype(jnp.int32).reshape(1), (group_map == student_expert).astype(jnp.int32)])

    meta = jnp.concatenate([router_weight[:, None], initial_id.astype(BF), jnp.zeros((12, META - 2), BF)], axis=1)
    own = jnp.pad(jnp.concatenate([tokens, meta], axis=1), ((0, 4), (0, 0)))
    a32, b16 = line_up(place, [own] + [shift(own, FIRST, by) for by in (1, 2, 3)])
    near, far = grow(a32, b16)

    weights = (teacher_gate, teacher_up, student_gate, student_up)
    h_near, ab_near = forward(info, near, *weights)
    h_far, ab_far = forward(info, far, *weights)
    far_out = down(h_far, student_down, teacher_down)
    near_out = down(h_near, student_down, teacher_down)

    rows48 = shrink(near_out, far_out)
    part = rows48.astype(BF)
    for by in (1, 2, 3):
        rows48 = rows48 + shift(part, FIRST, by).astype(F32)
    depth = tokens.shape[1]
    weight = join(a32[:, depth : depth + 1], b16[:, depth : depth + 1]).astype(F32)
    cotangent = (weight * (weight * rows48) * (1.0 / math.sqrt(total))).astype(BF)
    c_near, c_far = grow(cotangent[:32], cotangent[32:])

    send, keep = backward(
        core.astype(jnp.int32).reshape(1), near + far, c_near + c_far, student_down, h_near, h_far, ab_near, ab_far
    )
    got = lax.ppermute(send, "dp", [(0, 1), (1, 0)])
    return tuple(finish(keep, got))


def solution(mesh):
    placed = (
        P(("dp", "expert"), None),
        P(("dp", "expert")),
        P(("dp", "expert"), None),
        P(),
        P(None, "expert"),
        P(None, "expert"),
        P("expert", None),
        P(None, "expert"),
        P(None, "expert"),
        P("expert", None),
    )
    return jax.shard_map(
        per_device,
        mesh=mesh,
        in_specs=placed,
        out_specs=(P("dp", "expert"), P("dp", "expert"), P("expert", "dp")),
        check_vma=False,
    )
```

```python
import functools
import math

import jax
import jax.numpy as jnp
from jax import lax
from jax.experimental import pallas as pl
from jax.experimental.pallas import tpu as pltpu
from jax.sharding import PartitionSpec as P

F = 4096
E_ORIG = 4
META = 128
BF = jnp.bfloat16
F32 = jnp.float32
AXES = ("dp", "expert")
SIDE = 4


def coords(device):
    return device // 64, {"z": (device // 16) % SIDE, "y": (device // 4) % SIDE, "x": device % SIDE}


def number(core, at):
    return core * 64 + at["z"] * 16 + at["y"] * 4 + at["x"]


def join(*parts):
    return jnp.concatenate(parts, axis=0)


ORDERS = (("x", "y", "z"), ("y", "z", "x"), ("z", "x", "y"))
PIECES = range(3)
CROSS = (3, 5)


def step_pairs(piece, step):
    axis, pairs = ORDERS[piece][step // 2], []
    for device in range(128):
        core, at = coords(device)
        bits = (1, 3)[(step + core) % 2]
        pairs.append((device, number(core ^ (step in CROSS), {**at, axis: at[axis] ^ bits})))
    return pairs


def hop(value, piece, step):
    return lax.ppermute(value, AXES, step_pairs(piece, step))


def hop_back(value, piece, step):
    return lax.ppermute(value, AXES, [(to, own) for own, to in step_pairs(piece, step)])


def together(values):
    return lax.optimization_barrier(tuple(values))


def grow(parts):
    for step in (3, 4):
        parts = [join(v, hop(v, p, step)) for p, v in enumerate(parts)]
    return parts, [hop(v, p, 5) for p, v in enumerate(parts)]


def add(mine, got):
    return mine.astype(F32) + got.astype(F32)


def shrink(near, far):
    sums = []
    for p in PIECES:
        mine, theirs = near[p], far[p]
        for step in (5, 4, 3):
            got = hop_back(theirs.astype(BF), p, step)
            half = mine.shape[0] // 2
            if step > 3:
                theirs, mine = add(mine[half:], got[half:]), add(mine[:half], got[:half])
            else:
                mine = add(mine, got)
        sums.append(mine)
    for step in (2, 1, 0):
        sums = [add(v, hop(v.astype(BF), p, step)) for p, v in enumerate(sums)]
    return sums


def line_up_kernel(place_ref, mine, got, out):
    row = lax.broadcasted_iota(jnp.int32, (16, 32), 0)
    column = lax.broadcasted_iota(jnp.int32, (16, 32), 1)
    block, token = column // 8, column % 8
    place = jnp.zeros((16, 32), jnp.int32)
    for i in range(SIDE):
        place = jnp.where(block == i, place_ref[i], place)
    pick = jnp.where((row == place * 4 + token) & (token < 4), 1.0, 0.0).astype(BF)
    rows = jnp.concatenate([mine[...], got[...]], axis=0)
    out[...] = jnp.dot(pick, rows, preferred_element_type=F32).astype(BF)


def line_up(places, mine, got):
    vmem = pl.BlockSpec(memory_space=pltpu.VMEM)
    return pl.pallas_call(
        line_up_kernel,
        out_shape=jax.ShapeDtypeStruct((16, mine.shape[1]), BF),
        in_specs=[pl.BlockSpec(memory_space=pltpu.SMEM), vmem, vmem],
        out_specs=vmem,
        compiler_params=pltpu.CompilerParams(vmem_limit_bytes=32 << 20),
    )(places, mine, got)


def first_gather(own, core, at):
    parts = []
    for p in PIECES:
        mine = jnp.pad(own[4 * p : 4 * p + 4], ((0, 4), (0, 0)))
        mine = join(mine, hop(mine, p, 0))
        got = hop(mine, p, 1)
        flips = jnp.where(core == 0, jnp.array([0, 1, 3, 2]), jnp.array([0, 3, 1, 2])).astype(jnp.int32)
        rows = line_up(at[ORDERS[p][0]] ^ flips, mine, got)
        got = hop(rows, p, 2)
        place = at[ORDERS[p][1]]
        low = place < (place ^ jnp.where(core == 0, 1, 3))
        parts.append(join(jnp.where(low, rows, got), jnp.where(low, got, rows)))
    return parts


def forward_kernel(count, steps, info, *refs):
    xs, metas = refs[:count], refs[count : 2 * count]
    tg, tu, sg, su, h_ref, ab_ref, acc = refs[2 * count :]
    step = pl.program_id(0)
    x = jnp.concatenate([r[...] for r in xs], axis=0)
    w = jnp.concatenate([tg[...], tu[...], sg[...], su[...]], axis=1)
    part = jnp.dot(x, w, preferred_element_type=F32)

    @pl.when(step == 0)
    def _():
        acc[...] = part

    @pl.when(step > 0)
    def _():
        acc[...] += part

    @pl.when(step == steps - 1)
    def _():
        ids = jnp.concatenate([r[:, 1:2] for r in metas], axis=0).astype(F32)
        mask_t = ids == info[0].astype(F32)
        mask_s = jnp.zeros(ids.shape, F32)
        for i in range(E_ORIG):
            mask_s = mask_s + jnp.where(ids == float(i), info[1 + i].astype(F32), 0.0)
        mask_s = mask_s > 0.5
        gate, up = acc[:, 0:256], acc[:, 256:512]
        hid_t = gate * jax.nn.sigmoid(gate) * up
        h_ref[:, 128:384] = jnp.where(mask_t, -hid_t, 0.0).astype(BF)
        gate, up = acc[:, 512:640], acc[:, 640:768]
        sig = jax.nn.sigmoid(gate)
        silu = gate * sig
        h_ref[:, 0:128] = jnp.where(mask_s, silu * up, 0.0).astype(BF)
        ab_ref[:, 0:128] = jnp.where(mask_s, up * sig * (1.0 + gate * (1.0 - sig)), 0.0)
        ab_ref[:, 128:256] = jnp.where(mask_s, silu, 0.0)


def forward(info, chunks, tg, tu, sg, su):
    count, depth = len(chunks), tg.shape[0]
    rows, block = 128 * count, 1280
    steps = depth // block
    at_k = lambda k: (k, 0)
    return pl.pallas_call(
        functools.partial(forward_kernel, count, steps),
        grid=(steps,),
        out_shape=[jax.ShapeDtypeStruct((rows, 384), BF), jax.ShapeDtypeStruct((rows, 256), F32)],
        in_specs=[pl.BlockSpec(memory_space=pltpu.SMEM)]
        + [pl.BlockSpec((128, block), lambda k: (0, k))] * count
        + [pl.BlockSpec((128, META), lambda k: (0, depth // META))] * count
        + [pl.BlockSpec((block, w.shape[1]), at_k) for w in (tg, tu, sg, su)],
        out_specs=[pl.BlockSpec((rows, 384), lambda k: (0, 0)), pl.BlockSpec((rows, 256), lambda k: (0, 0))],
        scratch_shapes=[pltpu.VMEM((rows, 768), F32)],
        compiler_params=pltpu.CompilerParams(vmem_limit_bytes=40 << 20),
        cost_estimate=pl.CostEstimate(flops=2 * rows * depth * 768, bytes_accessed=2 * depth * (rows + 768), transcendentals=0),
    )(info, *chunks, *chunks, tg, tu, sg, su)


def down_kernel(count, h_ref, sd, td, *outs):
    w = jnp.concatenate([sd[...], td[...]], axis=0)
    out = jnp.dot(h_ref[...], w, preferred_element_type=F32).astype(BF)
    for i in range(count):
        outs[i][...] = out[128 * i : 128 * (i + 1)]


def down(hidden, sd, td):
    rows, width = hidden.shape[0], sd.shape[1]
    count, block = rows // 128, 1280
    return pl.pallas_call(
        functools.partial(down_kernel, count),
        grid=(width // block,),
        out_shape=[jax.ShapeDtypeStruct((128, width), BF)] * count,
        in_specs=[
            pl.BlockSpec((rows, 384), lambda n: (0, 0)),
            pl.BlockSpec((128, block), lambda n: (0, n)),
            pl.BlockSpec((256, block), lambda n: (0, n)),
        ],
        out_specs=[pl.BlockSpec((128, block), lambda n: (0, n))] * count,
        compiler_params=pltpu.CompilerParams(vmem_limit_bytes=40 << 20),
        cost_estimate=pl.CostEstimate(flops=2 * rows * width * 384, bytes_accessed=2 * width * (rows + 384), transcendentals=0),
    )(hidden, sd, td)


def backward_kernel(count, half, core, *refs):
    xs, cs = refs[:count], refs[count : 2 * count]
    sd, h1, h2, ab1, ab2, send, keep, acc, gt, ht = refs[2 * count :]
    step = pl.program_id(0)
    c = jnp.concatenate([r[...] for r in cs], axis=0)

    @pl.when(step < 2 * half)
    def _():
        part = lax.dot_general(c, sd[...], (((1,), (1,)), ((), ())), preferred_element_type=F32)

        @pl.when(step == 0)
        def _():
            acc[...] = part

        @pl.when(step > 0)
        def _():
            acc[...] += part

    @pl.when(step == 2 * half - 1)
    def _():
        ab = jnp.concatenate([ab1[...], ab2[...]], axis=0)
        gt[0:128, :] = (acc[...] * ab[:, 0:128]).T.astype(BF)
        gt[128:256, :] = (acc[...] * ab[:, 128:256]).T.astype(BF)
        ht[...] = jnp.concatenate([h1[...], h2[...]], axis=0).astype(F32).T.astype(BF)

    @pl.when(step >= 2 * half)
    def _():
        x = jnp.concatenate([r[...] for r in xs], axis=0)
        out = jnp.concatenate(
            [jnp.dot(gt[...], x, preferred_element_type=F32), jnp.dot(ht[...], c, preferred_element_type=F32)],
            axis=0,
        )

        @pl.when(step < 3 * half)
        def _():
            send[...] = out.astype(BF)

        @pl.when(step >= 3 * half)
        def _():
            keep[...] = out


def backward(core, xs, cs, sd, h1, h2, ab1, ab2):
    count, width = len(xs), sd.shape[1]
    rows, block = 128 * count, 1280
    half = width // block // 2
    turn = lambda s, core: lax.rem(s + (1 - core[0]) * half, 2 * half)
    x_at = lambda s, core: (0, turn(jnp.maximum(s, 2 * half), core))
    c_at = lambda s, core: (0, turn(s, core))
    d_at = lambda s, core: (0, turn(jnp.minimum(s, 2 * half - 1), core))
    whole = lambda s, core: (0, 0)
    return pl.pallas_call(
        functools.partial(backward_kernel, count, half),
        grid_spec=pltpu.PrefetchScalarGridSpec(
            num_scalar_prefetch=1,
            grid=(4 * half,),
            in_specs=[pl.BlockSpec((128, block), x_at)] * count
            + [pl.BlockSpec((128, block), c_at)] * count
            + [pl.BlockSpec((128, block), d_at)]
            + [pl.BlockSpec((rows // 2, 128), whole)] * 2
            + [pl.BlockSpec((rows // 2, 256), whole)] * 2,
            out_specs=[
                pl.BlockSpec((384, block), lambda s, core: (0, jnp.clip(s - 2 * half, 0, half - 1))),
                pl.BlockSpec((384, block), lambda s, core: (0, jnp.maximum(s - 3 * half, 0))),
            ],
            scratch_shapes=[pltpu.VMEM((rows, 128), F32), pltpu.VMEM((256, rows), BF), pltpu.VMEM((128, rows), BF)],
        ),
        out_shape=[jax.ShapeDtypeStruct((384, width // 2), BF), jax.ShapeDtypeStruct((384, width // 2), F32)],
        compiler_params=pltpu.CompilerParams(vmem_limit_bytes=48 << 20),
        cost_estimate=pl.CostEstimate(flops=2 * rows * width * 512, bytes_accessed=6 * rows * width, transcendentals=0),
    )(core, *xs, *cs, sd, h1, h2, ab1, ab2)


def finish_kernel(keep, got, gate, up, low):
    out = keep[...] + got[...].astype(F32)
    gate[...] = out[0:128].T
    up[...] = out[128:256].T
    low[...] = out[256:384]


def finish(keep, got):
    width, block = keep.shape[1], 512
    wide = pl.BlockSpec((384, block), lambda n: (0, n))
    tall = pl.BlockSpec((block, 128), lambda n: (n, 0))
    return pl.pallas_call(
        finish_kernel,
        grid=(width // block,),
        out_shape=[jax.ShapeDtypeStruct((width, 128), F32)] * 2 + [jax.ShapeDtypeStruct((128, width), F32)],
        in_specs=[wide, wide],
        out_specs=[tall, tall, pl.BlockSpec((128, block), lambda n: (0, n))],
        compiler_params=pltpu.CompilerParams(vmem_limit_bytes=32 << 20),
    )(keep, got)


def per_device(
    tokens,
    router_weight,
    initial_id,
    group_map,
    teacher_gate,
    teacher_up,
    teacher_down,
    student_gate,
    student_up,
    student_down,
):
    core, owner = lax.axis_index("dp"), lax.axis_index("expert")
    total = tokens.shape[0] * 128
    at = {"z": owner // 16, "y": (owner // SIDE) % SIDE, "x": owner % SIDE}
    teacher_expert = owner * teacher_gate.shape[1] // F
    student_expert = owner * student_gate.shape[1] // F
    info = jnp.concatenate([teacher_expert.astype(jnp.int32).reshape(1), (group_map == student_expert).astype(jnp.int32)])

    meta = jnp.concatenate([router_weight[:, None], initial_id.astype(BF), jnp.zeros((12, META - 2), BF)], axis=1)
    parts = first_gather(jnp.concatenate([tokens, meta], axis=1), core, at)
    near, far = grow(parts)

    weights = (teacher_gate, teacher_up, student_gate, student_up)
    h_near, ab_near = forward(info, near, *weights)
    far, h_near = lax.optimization_barrier((far, h_near))
    h_far, ab_far = forward(info, far, *weights)
    far_out = down(h_far, student_down, teacher_down)
    near_out = down(h_near, student_down, teacher_down)

    depth, scale = tokens.shape[1], 1.0 / math.sqrt(total)
    cotangent = []
    for part, rows in zip(parts, shrink(near_out, far_out)):
        weight = part[:, depth : depth + 1].astype(F32)
        cotangent.append((weight * (weight * rows) * scale).astype(BF))
    c_near, c_far = grow(cotangent)

    send, keep = backward(
        core.astype(jnp.int32).reshape(1), near + far, c_near + c_far, student_down, h_near, h_far, ab_near, ab_far
    )
    got = lax.ppermute(send, "dp", [(0, 1), (1, 0)])
    return tuple(finish(keep, got))


def solution(mesh):
    placed = (
        P(("dp", "expert"), None),
        P(("dp", "expert")),
        P(("dp", "expert"), None),
        P(),
        P(None, "expert"),
        P(None, "expert"),
        P("expert", None),
        P(None, "expert"),
        P(None, "expert"),
        P("expert", None),
    )
    return jax.shard_map(
        per_device,
        mesh=mesh,
        in_specs=placed,
        out_specs=(P("dp", "expert"), P("dp", "expert"), P("expert", "dp")),
        check_vma=False,
    )
```

```python
import functools
import math

import jax
import jax.numpy as jnp
from jax import lax
from jax.experimental import pallas as pl
from jax.experimental.pallas import tpu as pltpu
from jax.sharding import PartitionSpec as P

F = 4096
E_ORIG = 4
META = 128
BF = jnp.bfloat16
F32 = jnp.float32
AXES = ("dp", "expert")
SIDE = 4


def coords(device):
    return device // 64, {"z": (device // 16) % SIDE, "y": (device // 4) % SIDE, "x": device % SIDE}


def number(core, at):
    return core * 64 + at["z"] * 16 + at["y"] * 4 + at["x"]


def join(*parts):
    return jnp.concatenate(parts, axis=0)


ORDERS = (("x", "y", "z"), ("y", "z", "x"), ("z", "x", "y"))
PIECES = range(3)
CROSS = (3, 5)


def step_pairs(piece, step):
    axis, pairs = ORDERS[piece][step // 2], []
    for device in range(128):
        core, at = coords(device)
        bits = (1, 3)[(step + core) % 2]
        pairs.append((device, number(core ^ (step in CROSS), {**at, axis: at[axis] ^ bits})))
    return pairs


def hop(value, piece, step):
    return lax.ppermute(value, AXES, step_pairs(piece, step))


def hop_back(value, piece, step):
    return lax.ppermute(value, AXES, [(to, own) for own, to in step_pairs(piece, step)])


def together(values):
    return lax.optimization_barrier(tuple(values))


def grow(parts):
    for step in (3, 4):
        parts = [join(v, hop(v, p, step)) for p, v in enumerate(parts)]
    return parts, [hop(v, p, 5) for p, v in enumerate(parts)]


def add(mine, got):
    return mine.astype(F32) + got.astype(F32)


def shrink(near, far):
    sums = []
    for p in PIECES:
        mine, theirs = near[p], far[p]
        for step in (5, 4, 3):
            got = hop_back(theirs.astype(BF), p, step)
            half = mine.shape[0] // 2
            if step > 3:
                theirs, mine = add(mine[half:], got[half:]), add(mine[:half], got[:half])
            else:
                mine = add(mine, got)
        sums.append(mine)
    for step in (2, 1, 0):
        sums = [add(v, hop(v.astype(BF), p, step)) for p, v in enumerate(sums)]
    return lax.optimization_barrier(sums)


def line_up_kernel(place_ref, mine, got, out):
    row = lax.broadcasted_iota(jnp.int32, (16, 32), 0)
    column = lax.broadcasted_iota(jnp.int32, (16, 32), 1)
    block, token = column // 8, column % 8
    place = jnp.zeros((16, 32), jnp.int32)
    for i in range(SIDE):
        place = jnp.where(block == i, place_ref[i], place)
    pick = jnp.where((row == place * 4 + token) & (token < 4), 1.0, 0.0).astype(BF)
    rows = jnp.concatenate([mine[...], got[...]], axis=0)
    out[...] = jnp.dot(pick, rows, preferred_element_type=F32).astype(BF)


def line_up(places, mine, got):
    vmem = pl.BlockSpec(memory_space=pltpu.VMEM)
    return pl.pallas_call(
        line_up_kernel,
        out_shape=jax.ShapeDtypeStruct((16, mine.shape[1]), BF),
        in_specs=[pl.BlockSpec(memory_space=pltpu.SMEM), vmem, vmem],
        out_specs=vmem,
        compiler_params=pltpu.CompilerParams(vmem_limit_bytes=16 << 20),
    )(places, mine, got)


def first_gather(own, core, at):
    parts = []
    for p in PIECES:
        mine = jnp.pad(own[4 * p : 4 * p + 4], ((0, 4), (0, 0)))
        mine = join(mine, hop(mine, p, 0))
        got = hop(mine, p, 1)
        flips = jnp.where(core == 0, jnp.array([0, 1, 3, 2]), jnp.array([0, 3, 1, 2])).astype(jnp.int32)
        rows = line_up(at[ORDERS[p][0]] ^ flips, mine, got)
        got = hop(rows, p, 2)
        place = at[ORDERS[p][1]]
        low = place < (place ^ jnp.where(core == 0, 1, 3))
        parts.append(join(jnp.where(low, rows, got), jnp.where(low, got, rows)))
    return parts


def forward_kernel(count, steps, info, *refs):
    xs, metas = refs[:count], refs[count : 2 * count]
    tg, tu, sg, su, h_ref, ht_ref, ab_ref, acc = refs[2 * count :]
    step = pl.program_id(0)
    x = jnp.concatenate([r[...] for r in xs], axis=0)
    w = jnp.concatenate([tg[...], tu[...], sg[...], su[...]], axis=1)
    part = jnp.dot(x, w, preferred_element_type=F32)

    @pl.when(step == 0)
    def _():
        acc[...] = part

    @pl.when(step > 0)
    def _():
        acc[...] += part

    @pl.when(step == steps - 1)
    def _():
        ids = jnp.concatenate([r[:, 1:2] for r in metas], axis=0).astype(F32)
        mask_t = ids == info[0].astype(F32)
        mask_s = jnp.zeros(ids.shape, F32)
        for i in range(E_ORIG):
            mask_s = mask_s + jnp.where(ids == float(i), info[1 + i].astype(F32), 0.0)
        mask_s = mask_s > 0.5
        gate, up = acc[:, 0:256], acc[:, 256:512]
        hid_t = gate * jax.nn.sigmoid(gate) * up
        h_ref[:, 128:384] = jnp.where(mask_t, -hid_t, 0.0).astype(BF)
        gate, up = acc[:, 512:640], acc[:, 640:768]
        sig = jax.nn.sigmoid(gate)
        silu = gate * sig
        hid_s = jnp.where(mask_s, silu * up, 0.0)
        h_ref[:, 0:128] = hid_s.astype(BF)
        ht_ref[...] = hid_s.T.astype(BF)
        ab_ref[:, 0:128] = jnp.where(mask_s, up * sig * (1.0 + gate * (1.0 - sig)), 0.0)
        ab_ref[:, 128:256] = jnp.where(mask_s, silu, 0.0)


def forward(info, chunks, tg, tu, sg, su):
    count, depth = len(chunks), tg.shape[0]
    rows, block = 128 * count, 1280
    steps = depth // block
    at_k = lambda k: (k, 0)
    return pl.pallas_call(
        functools.partial(forward_kernel, count, steps),
        grid=(steps,),
        out_shape=[
            jax.ShapeDtypeStruct((rows, 384), BF),
            jax.ShapeDtypeStruct((128, rows), BF),
            jax.ShapeDtypeStruct((rows, 256), F32),
        ],
        in_specs=[pl.BlockSpec(memory_space=pltpu.SMEM)]
        + [pl.BlockSpec((128, block), lambda k: (0, k))] * count
        + [pl.BlockSpec((128, META), lambda k: (0, depth // META))] * count
        + [pl.BlockSpec((block, w.shape[1]), at_k) for w in (tg, tu, sg, su)],
        out_specs=[
            pl.BlockSpec((rows, 384), lambda k: (0, 0)),
            pl.BlockSpec((128, rows), lambda k: (0, 0)),
            pl.BlockSpec((rows, 256), lambda k: (0, 0)),
        ],
        scratch_shapes=[pltpu.VMEM((rows, 768), F32)],
        compiler_params=pltpu.CompilerParams(vmem_limit_bytes=16 << 20),
        cost_estimate=pl.CostEstimate(flops=2 * rows * depth * 768, bytes_accessed=2 * depth * (rows + 768), transcendentals=0),
    )(info, *chunks, *chunks, tg, tu, sg, su)


def down_kernel(count, h_ref, sd, td, *outs):
    w = jnp.concatenate([sd[...], td[...]], axis=0)
    out = jnp.dot(h_ref[...], w, preferred_element_type=F32).astype(BF)
    for i in range(count):
        outs[i][...] = out[128 * i : 128 * (i + 1)]


def down(hidden, sd, td):
    rows, width = hidden.shape[0], sd.shape[1]
    count, block = rows // 128, 1280
    return pl.pallas_call(
        functools.partial(down_kernel, count),
        grid=(width // block,),
        out_shape=[jax.ShapeDtypeStruct((128, width), BF)] * count,
        in_specs=[
            pl.BlockSpec((rows, 384), lambda n: (0, 0)),
            pl.BlockSpec((128, block), lambda n: (0, n)),
            pl.BlockSpec((256, block), lambda n: (0, n)),
        ],
        out_specs=[pl.BlockSpec((128, block), lambda n: (0, n))] * count,
        compiler_params=pltpu.CompilerParams(vmem_limit_bytes=16 << 20),
        cost_estimate=pl.CostEstimate(flops=2 * rows * width * 384, bytes_accessed=2 * width * (rows + 384), transcendentals=0),
    )(hidden, sd, td)


BLOCK = 1280


def into(acc, step, part):
    @pl.when(step == 0)
    def _():
        acc[...] = part

    @pl.when(step > 0)
    def _():
        acc[...] += part


def dhidden_part(cs, sd):
    c = jnp.concatenate([r[...] for r in cs], axis=0)
    return lax.dot_general(c, sd[...], (((1,), (1,)), ((), ())), preferred_element_type=F32)


def dgates(acc, ab):
    return jnp.concatenate([acc[...] * ab[:, 0:128], acc[...] * ab[:, 128:256]], axis=1).astype(BF)


def dhidden_kernel(steps, *refs):
    cs, (sd, ab, g, acc) = refs[:-4], refs[-4:]
    step = pl.program_id(0)
    into(acc, step, dhidden_part(cs, sd))

    @pl.when(step == steps - 1)
    def _():
        g[...] = dgates(acc, ab)


def dhidden(cs, sd, ab):
    rows, width = 128 * len(cs), sd.shape[1]
    steps = width // BLOCK
    wide = pl.BlockSpec((128, BLOCK), lambda k: (0, k))
    whole = pl.BlockSpec((rows, 256), lambda k: (0, 0))
    return pl.pallas_call(
        functools.partial(dhidden_kernel, steps),
        grid=(steps,),
        out_shape=jax.ShapeDtypeStruct((rows, 256), BF),
        in_specs=[wide] * len(cs) + [wide, whole],
        out_specs=whole,
        scratch_shapes=[pltpu.VMEM((rows, 128), F32)],
        compiler_params=pltpu.CompilerParams(vmem_limit_bytes=16 << 20),
        cost_estimate=pl.CostEstimate(flops=2 * rows * width * 128, bytes_accessed=2 * rows * width, transcendentals=0),
    )(*cs, sd, ab)


def turn_kernel(*refs):
    xs, out = refs[:-1], refs[-1]
    for i, r in enumerate(xs):
        out[:, 128 * i : 128 * (i + 1)] = r[...].T


def turn(xs, width):
    rows, block = 128 * len(xs), 1280
    return pl.pallas_call(
        turn_kernel,
        grid=(width // block,),
        out_shape=jax.ShapeDtypeStruct((width, rows), BF),
        in_specs=[pl.BlockSpec((128, block), lambda n: (0, n))] * len(xs),
        out_specs=pl.BlockSpec((block, rows), lambda n: (n, 0)),
        compiler_params=pltpu.CompilerParams(vmem_limit_bytes=16 << 20),
        cost_estimate=pl.CostEstimate(flops=0, bytes_accessed=4 * rows * width, transcendentals=0),
    )(*xs)


def products(xt, cs, g, ht):
    c = jnp.concatenate([r[...] for r in cs], axis=0)
    return jnp.dot(xt[...], g, preferred_element_type=F32), jnp.dot(ht, c, preferred_element_type=F32)


def send_kernel(half, core, *refs):
    cs = refs[0:6]
    xt, sd, g1, ht1, ht2, ab, tall, low, g2, acc = refs[6:]
    step = pl.program_id(0)

    @pl.when(step < 2 * half)
    def _():
        into(acc, step, dhidden_part(cs[3:], sd))

    @pl.when(step == 2 * half - 1)
    def _():
        g2[...] = dgates(acc, ab)

    @pl.when(step >= 2 * half)
    def _():
        g = jnp.concatenate([g1[...], g2[...]], axis=0)
        ht = jnp.concatenate([ht1[...], ht2[...]], axis=1)
        up, down = products(xt, cs, g, ht)
        tall[...] = up.astype(BF)
        low[...] = down.astype(BF)


def send_half(core, xt, cs, sd, g1, ht1, ht2, ab):
    width = sd.shape[1]
    half = width // BLOCK // 2
    theirs = lambda s, core: (1 - core[0]) * half + jnp.maximum(s - 2 * half, 0)
    at = lambda s, core: (0, theirs(s, core))
    far_at = lambda s, core: (0, jnp.where(s < 2 * half, s, theirs(s, core)))
    out_at = lambda s: jnp.maximum(s - 2 * half, 0)
    fixed = lambda *shape: pl.BlockSpec(shape, lambda s, core: (0, 0))
    return pl.pallas_call(
        functools.partial(send_kernel, half),
        grid_spec=pltpu.PrefetchScalarGridSpec(
            num_scalar_prefetch=1,
            grid=(3 * half,),
            in_specs=[pl.BlockSpec((128, BLOCK), at)] * 3
            + [pl.BlockSpec((128, BLOCK), far_at)] * 3
            + [pl.BlockSpec((BLOCK, 768), lambda s, core: (theirs(s, core), 0))]
            + [pl.BlockSpec((128, BLOCK), lambda s, core: (0, jnp.minimum(s, 2 * half - 1)))]
            + [fixed(384, 256), fixed(128, 384), fixed(128, 384), fixed(384, 256)],
            out_specs=[
                pl.BlockSpec((BLOCK, 256), lambda s, core: (out_at(s), 0)),
                pl.BlockSpec((128, BLOCK), lambda s, core: (0, out_at(s))),
                fixed(384, 256),
            ],
            scratch_shapes=[pltpu.VMEM((384, 128), F32)],
        ),
        out_shape=[
            jax.ShapeDtypeStruct((width // 2, 256), BF),
            jax.ShapeDtypeStruct((128, width // 2), BF),
            jax.ShapeDtypeStruct((384, 256), BF),
        ],
        compiler_params=pltpu.CompilerParams(vmem_limit_bytes=16 << 20),
        cost_estimate=pl.CostEstimate(flops=768 * width * 512, bytes_accessed=4 * 768 * width, transcendentals=0),
    )(core, *cs, xt, sd, g1, ht1, ht2, ab)


def keep_kernel(core, *refs):
    cs = refs[0:6]
    xt, g1, g2, ht1, ht2, tall, low = refs[6:]
    g = jnp.concatenate([g1[...], g2[...]], axis=0)
    ht = jnp.concatenate([ht1[...], ht2[...]], axis=1)
    tall[...], low[...] = products(xt, cs, g, ht)


def keep_half(core, xt, cs, g1, g2, ht1, ht2):
    width = cs[0].shape[1] // 2
    steps = width // BLOCK
    fixed = lambda *shape: pl.BlockSpec(shape, lambda s, core: (0, 0))
    return pl.pallas_call(
        keep_kernel,
        grid_spec=pltpu.PrefetchScalarGridSpec(
            num_scalar_prefetch=1,
            grid=(steps,),
            in_specs=[pl.BlockSpec((128, BLOCK), lambda s, core: (0, core[0] * steps + s))] * 6
            + [pl.BlockSpec((BLOCK, 768), lambda s, core: (core[0] * steps + s, 0))]
            + [fixed(384, 256)] * 2
            + [fixed(128, 384)] * 2,
            out_specs=[
                pl.BlockSpec((BLOCK, 256), lambda s, core: (s, 0)),
                pl.BlockSpec((128, BLOCK), lambda s, core: (0, s)),
            ],
        ),
        out_shape=[jax.ShapeDtypeStruct((width, 256), F32), jax.ShapeDtypeStruct((128, width), F32)],
        compiler_params=pltpu.CompilerParams(vmem_limit_bytes=16 << 20),
        cost_estimate=pl.CostEstimate(flops=768 * width * 768, bytes_accessed=4 * 768 * width, transcendentals=0),
    )(core, *cs, xt, g1, g2, ht1, ht2)


def per_device(
    tokens,
    router_weight,
    initial_id,
    group_map,
    teacher_gate,
    teacher_up,
    teacher_down,
    student_gate,
    student_up,
    student_down,
):
    core, owner = lax.axis_index("dp"), lax.axis_index("expert")
    total = tokens.shape[0] * 128
    at = {"z": owner // 16, "y": (owner // SIDE) % SIDE, "x": owner % SIDE}
    teacher_expert = owner * teacher_gate.shape[1] // F
    student_expert = owner * student_gate.shape[1] // F
    info = jnp.concatenate([teacher_expert.astype(jnp.int32).reshape(1), (group_map == student_expert).astype(jnp.int32)])

    meta = jnp.concatenate([router_weight[:, None], initial_id.astype(BF), jnp.zeros((12, META - 2), BF)], axis=1)
    parts = first_gather(jnp.concatenate([tokens, meta], axis=1), core, at)
    near, far = (v[::-1] for v in grow(parts))

    weights = (teacher_gate, teacher_up, student_gate, student_up)
    h_near, ht_near, ab_near = forward(info, near, *weights)
    far, h_near = lax.optimization_barrier((far, h_near))
    h_far, ht_far, ab_far = forward(info, far, *weights)
    far_out = down(h_far, student_down, teacher_down)
    near_out = down(h_near, student_down, teacher_down)

    depth, scale = tokens.shape[1], 1.0 / math.sqrt(total)
    xt = turn(near + far, depth)
    cotangent = []
    for part, rows in zip(parts, shrink(near_out[::-1], far_out[::-1])):
        weight = part[:, depth : depth + 1].astype(F32)
        cotangent.append((weight * (weight * rows) * scale).astype(BF))
    c_near, c_far = (v[::-1] for v in grow(cotangent))

    g_near = dhidden(c_near, student_down, ab_near)
    c_far, g_near = lax.optimization_barrier((c_far, g_near))
    side, cs = core.astype(jnp.int32).reshape(1), c_near + c_far
    *send, g_far = send_half(side, xt, cs, student_down, g_near, ht_near, ht_far, ab_far)
    tall_got, low_got = (lax.ppermute(v, "dp", [(0, 1), (1, 0)]) for v in send)
    tall, low = keep_half(side, xt, cs, g_near, g_far, ht_near, ht_far)
    tall, low = tall + tall_got.astype(F32), low + low_got.astype(F32)
    return tall[:, 0:128], tall[:, 128:256], low


def solution(mesh):
    placed = (
        P(("dp", "expert"), None),
        P(("dp", "expert")),
        P(("dp", "expert"), None),
        P(),
        P(None, "expert"),
        P(None, "expert"),
        P("expert", None),
        P(None, "expert"),
        P(None, "expert"),
        P("expert", None),
    )
    return jax.shard_map(
        per_device,
        mesh=mesh,
        in_specs=placed,
        out_specs=(P("dp", "expert"), P("dp", "expert"), P("expert", "dp")),
        check_vma=False,
    )
```

```python
import functools
import math

import jax
import jax.numpy as jnp
from jax import lax
from jax.experimental import pallas as pl
from jax.experimental.pallas import tpu as pltpu
from jax.sharding import PartitionSpec as P

F = 4096
E_ORIG = 4
META = 128
BLOCK = 1280
BF = jnp.bfloat16
F32 = jnp.float32
AXES = ("dp", "expert")
SIDE = 4


def coords(device):
    return device // 64, {"z": (device // 16) % SIDE, "y": (device // 4) % SIDE, "x": device % SIDE}


def number(core, at):
    return core * 64 + at["z"] * 16 + at["y"] * 4 + at["x"]


def join(*parts):
    return jnp.concatenate(parts, axis=0)


ORDERS = (("x", "y", "z"), ("y", "z", "x"), ("z", "x", "y"))
PIECES = range(3)
CROSS = (3, 5)


def step_pairs(piece, step):
    axis, pairs = ORDERS[piece][step // 2], []
    for device in range(128):
        core, at = coords(device)
        bits = (1, 3)[(step + core) % 2]
        pairs.append((device, number(core ^ (step in CROSS), {**at, axis: at[axis] ^ bits})))
    return pairs


def hop(value, piece, step):
    return lax.ppermute(value, AXES, step_pairs(piece, step))


def hop_back(value, piece, step):
    return lax.ppermute(value, AXES, [(to, own) for own, to in step_pairs(piece, step)])


def add(mine, got):
    return mine.astype(F32) + got.astype(F32)


def grow(parts, low):
    wide = []
    for p, rows in enumerate(parts):
        got = hop(rows, p, 2)
        wide.append(join(jnp.where(low[p], rows, got), jnp.where(low[p], got, rows)))
    for step in (3, 4):
        wide = [join(v, hop(v, p, step)) for p, v in enumerate(wide)]
    return wide[::-1], [hop(v, p, 5) for p, v in enumerate(wide)][::-1]


def shrink(near, far, low):
    sums = []
    for p in PIECES:
        mine, theirs = near[2 - p], far[2 - p]
        for step in (5, 4, 3):
            got = hop_back(theirs.astype(BF), p, step)
            half = mine.shape[0] // 2
            if step > 3:
                theirs, mine = add(mine[half:], got[half:]), add(mine[:half], got[:half])
            else:
                mine = add(mine, got)
        first, last = mine[:16], mine[16:]
        got = hop(jnp.where(low[p], last, first).astype(BF), p, 2)
        sums.append(add(jnp.where(low[p], first, last), got))
    for step in (1, 0):
        sums = [add(v, hop(v.astype(BF), p, step)) for p, v in enumerate(sums)]
    return lax.optimization_barrier(sums)


def line_up_kernel(place_ref, mine, got, out):
    row = lax.broadcasted_iota(jnp.int32, (16, 32), 0)
    column = lax.broadcasted_iota(jnp.int32, (16, 32), 1)
    block, token = column // 8, column % 8
    place = jnp.zeros((16, 32), jnp.int32)
    for i in range(SIDE):
        place = jnp.where(block == i, place_ref[i], place)
    pick = jnp.where((row == place * 4 + token) & (token < 4), 1.0, 0.0).astype(BF)
    rows = jnp.concatenate([mine[...], got[...]], axis=0)
    out[...] = jnp.dot(pick, rows, preferred_element_type=F32).astype(BF)


def line_up(places, mine, got):
    vmem = pl.BlockSpec(memory_space=pltpu.VMEM)
    return pl.pallas_call(
        line_up_kernel,
        out_shape=jax.ShapeDtypeStruct((16, mine.shape[1]), BF),
        in_specs=[pl.BlockSpec(memory_space=pltpu.SMEM), vmem, vmem],
        out_specs=vmem,
        compiler_params=pltpu.CompilerParams(vmem_limit_bytes=16 << 20),
    )(places, mine, got)


def pack_kernel(tokens, weight, ids, *outs):
    rows = tokens.shape[0]
    row = lax.broadcasted_iota(jnp.int32, (rows, rows), 0)
    diagonal = row == lax.broadcasted_iota(jnp.int32, (rows, rows), 1)
    column = lambda v: jnp.sum(jnp.where(diagonal, v.astype(F32), 0.0), axis=1, keepdims=True)
    place = lax.broadcasted_iota(jnp.int32, (rows, META), 1)
    meta = jnp.where(place == 0, column(weight[...]), jnp.where(place == 1, column(ids[...]), 0.0))
    both = jnp.concatenate([tokens[...].astype(F32), meta], axis=1)
    empty = jnp.zeros((4, both.shape[1]), F32)
    for i, out in enumerate(outs):
        out[...] = jnp.concatenate([both[4 * i : 4 * i + 4], empty], axis=0).astype(BF)


def pack(tokens, weight, ids):
    whole = lambda *shape: pl.BlockSpec(shape, lambda n: (0, 0))
    rows, width = tokens.shape
    return pl.pallas_call(
        pack_kernel,
        grid=(1,),
        out_shape=[jax.ShapeDtypeStruct((8, width + META), BF)] * 3,
        in_specs=[whole(rows, width), whole(1, rows), whole(1, rows)],
        out_specs=[whole(8, width + META)] * 3,
        compiler_params=pltpu.CompilerParams(vmem_limit_bytes=60 << 20),
    )(tokens, weight.reshape(1, -1), ids.reshape(1, -1))


def first_gather(blocks, core, at):
    flips = jnp.where(core == 0, jnp.array([0, 1, 3, 2]), jnp.array([0, 3, 1, 2])).astype(jnp.int32)
    parts = []
    for p, mine in enumerate(blocks):
        mine = join(mine, hop(mine, p, 0))
        parts.append(line_up(at[ORDERS[p][0]] ^ flips, mine, hop(mine, p, 1)))
    return parts


VMEM = pl.BlockSpec(memory_space=pltpu.VMEM)
SMEM = pl.BlockSpec(memory_space=pltpu.SMEM)
PARAMS = pltpu.CompilerParams(vmem_limit_bytes=16 << 20)


def shaped(*shape, dtype=BF):
    return jax.ShapeDtypeStruct(shape, dtype)


def dot(a, b):
    return jnp.dot(a, b, preferred_element_type=F32)


def forward_kernel(count, info, *refs):
    xs, (tg, tu, sg, su, sd, td) = refs[:count], refs[count : count + 6]
    outs, (h_ref, ab_ref, hidden) = refs[count + 6 : 2 * count + 6], refs[2 * count + 6 :]
    depth = tg.shape[0]
    for i, x_ref in enumerate(xs):
        rows = slice(128 * i, 128 * (i + 1))
        x = x_ref[:, 0:depth]
        ids = x_ref[:, depth : depth + META].astype(F32)[:, 1:2]
        mask_t = ids == info[0].astype(F32)
        mask_s = jnp.zeros(ids.shape, F32)
        for e in range(E_ORIG):
            mask_s = mask_s + jnp.where(ids == float(e), info[1 + e].astype(F32), 0.0)
        mask_s = mask_s > 0.5
        both = dot(x, jnp.concatenate([sg[...], su[...]], axis=1))
        gate, up = both[:, 0:128], both[:, 128:256]
        sig = jax.nn.sigmoid(gate)
        silu = gate * sig
        hid_s = jnp.where(mask_s, silu * up, 0.0)
        hidden[rows, 0:128] = hid_s.astype(BF)
        ab_ref[rows, 0:128] = jnp.where(mask_s, up * sig * (1.0 + gate * (1.0 - sig)), 0.0)
        ab_ref[rows, 128:256] = jnp.where(mask_s, silu, 0.0)
        gate, up = dot(x, tg[...]), dot(x, tu[...])
        hid_t = gate * jax.nn.sigmoid(gate) * up
        hidden[rows, 128:384] = jnp.where(mask_t, -hid_t, 0.0).astype(BF)
    for i, out in enumerate(outs):
        h = hidden[128 * i : 128 * (i + 1), :]
        for at in range(0, depth, BLOCK):
            n = slice(at, at + BLOCK)
            out[:, n] = dot(h, jnp.concatenate([sd[:, n], td[:, n]], axis=0)).astype(BF)
        h_ref[128 * i : 128 * (i + 1), :] = h[:, 0:128]


def forward(info, chunks, *weights):
    count, depth = len(chunks), weights[0].shape[0]
    rows = 128 * count
    *outs, h, ab = pl.pallas_call(
        functools.partial(forward_kernel, count),
        out_shape=[shaped(128, depth)] * count + [shaped(rows, 128), shaped(rows, 256, dtype=F32)],
        in_specs=[SMEM] + [VMEM] * (count + 6),
        out_specs=[VMEM] * (count + 2),
        scratch_shapes=[pltpu.VMEM((rows, 384), BF)],
        compiler_params=PARAMS,
        cost_estimate=pl.CostEstimate(flops=2 * rows * depth * 1152, bytes_accessed=2 * depth * (rows + 1152), transcendentals=0),
    )(info, *chunks, *weights)
    return outs, h, ab


def dgates(c, sd, ab):
    dhidden = lax.dot_general(c, sd, (((1,), (1,)), ((), ())), preferred_element_type=F32)
    return jnp.concatenate([dhidden * ab[:, 0:128], dhidden * ab[:, 128:256]], axis=1).astype(BF)


def dgates_kernel(*refs):
    cs, (sd, ab, g) = refs[:-3], refs[-3:]
    for i, c in enumerate(cs):
        rows = slice(128 * i, 128 * (i + 1))
        g[rows, :] = dgates(c[...], sd[...], ab[rows, :])


def gates_of(cs, sd, ab):
    rows = 128 * len(cs)
    return pl.pallas_call(
        dgates_kernel,
        out_shape=shaped(rows, 256),
        in_specs=[VMEM] * (len(cs) + 2),
        out_specs=VMEM,
        compiler_params=PARAMS,
        cost_estimate=pl.CostEstimate(flops=2 * rows * sd.size, bytes_accessed=2 * rows * sd.shape[1], transcendentals=0),
    )(*cs, sd, ab)


def turn_kernel(*refs):
    xs, (h1, h2, out, ht) = refs[:-4], refs[-4:]
    for i, r in enumerate(xs):
        out[:, 128 * i : 128 * (i + 1)] = r[...].T

    @pl.when(pl.program_id(0) == 0)
    def _():
        ht[...] = jnp.concatenate([h1[...].T, h2[...].T], axis=1)


def turn(xs, h1, h2, width):
    rows = 128 * len(xs)
    whole = lambda *shape: pl.BlockSpec(shape, lambda n: (0, 0))
    return pl.pallas_call(
        turn_kernel,
        grid=(width // BLOCK,),
        out_shape=[shaped(width, rows), shaped(128, rows)],
        in_specs=[pl.BlockSpec((128, BLOCK), lambda n: (0, n))] * len(xs) + [whole(rows // 2, 128)] * 2,
        out_specs=[pl.BlockSpec((BLOCK, rows), lambda n: (n, 0)), whole(128, rows)],
        compiler_params=PARAMS,
        cost_estimate=pl.CostEstimate(flops=0, bytes_accessed=4 * rows * width, transcendentals=0),
    )(*xs, h1, h2)


def products(side, xt, cs, g, ht, tall, low):
    width = low.shape[1]
    for at in range(0, width, BLOCK):
        here = pl.ds(pl.multiple_of(side * width + at, 128), BLOCK)
        tall[at : at + BLOCK, :] = dot(xt[here, :], g).astype(tall.dtype)
        total = None
        for i in range(0, len(cs), 2):
            c = jnp.concatenate([r[:, here] for r in cs[i : i + 2]], axis=0)
            part = dot(ht[:, 128 * i : 128 * (i + 2)], c)
            total = part if total is None else total + part
        low[:, at : at + BLOCK] = total.astype(low.dtype)


def send_kernel(core, *refs):
    cs, (xt, sd, g1, ht, ab, tall, low, g2) = refs[0:6], refs[6:]
    for i, c in enumerate(cs[3:]):
        rows = slice(128 * i, 128 * (i + 1))
        g2[rows, :] = dgates(c[...], sd[...], ab[rows, :])
    g = jnp.concatenate([g1[...], g2[...]], axis=0)
    products(1 - core[0], xt, cs, g, ht, tall, low)


def send_half(core, cs, xt, sd, g1, ht, ab):
    width = sd.shape[1]
    return pl.pallas_call(
        send_kernel,
        out_shape=[shaped(width // 2, 256), shaped(128, width // 2), shaped(384, 256)],
        in_specs=[SMEM] + [VMEM] * 11,
        out_specs=[VMEM] * 3,
        compiler_params=PARAMS,
        cost_estimate=pl.CostEstimate(flops=768 * width * 512, bytes_accessed=4 * 768 * width, transcendentals=0),
    )(core, *cs, xt, sd, g1, ht, ab)


def keep_kernel(core, *refs):
    cs, (xt, g1, g2, ht, tall, low) = refs[0:6], refs[6:]
    g = jnp.concatenate([g1[...], g2[...]], axis=0)
    products(core[0], xt, cs, g, ht, tall, low)


def keep_half(core, cs, xt, g1, g2, ht):
    width = cs[0].shape[1] // 2
    return pl.pallas_call(
        keep_kernel,
        out_shape=[shaped(width, 256, dtype=F32), shaped(128, width, dtype=F32)],
        in_specs=[SMEM] + [VMEM] * 10,
        out_specs=[VMEM] * 2,
        compiler_params=PARAMS,
        cost_estimate=pl.CostEstimate(flops=768 * width * 768, bytes_accessed=4 * 768 * width, transcendentals=0),
    )(core, *cs, xt, g1, g2, ht)


def per_device(
    tokens,
    router_weight,
    initial_id,
    group_map,
    teacher_gate,
    teacher_up,
    teacher_down,
    student_gate,
    student_up,
    student_down,
):
    core, owner = lax.axis_index("dp"), lax.axis_index("expert")
    total = tokens.shape[0] * 128
    at = {"z": owner // 16, "y": (owner // SIDE) % SIDE, "x": owner % SIDE}
    teacher_expert = owner * teacher_gate.shape[1] // F
    student_expert = owner * student_gate.shape[1] // F
    info = jnp.concatenate([teacher_expert.astype(jnp.int32).reshape(1), (group_map == student_expert).astype(jnp.int32)])

    low = []
    for order in ORDERS:
        place = at[order[1]]
        low.append(place < (place ^ jnp.where(core == 0, 1, 3)))
    parts = first_gather(pack(tokens, router_weight, initial_id), core, at)
    near, far = grow(parts, low)

    weights = (teacher_gate, teacher_up, student_gate, student_up, student_down, teacher_down)
    near_out, h_near, ab_near = forward(info, near, *weights)
    far, h_near = lax.optimization_barrier((far, h_near))
    far_out, h_far, ab_far = forward(info, far, *weights)

    depth, scale = tokens.shape[1], 1.0 / math.sqrt(total)
    xt, ht = turn(near + far, h_near, h_far, depth)
    cotangent = []
    for part, rows in zip(parts, shrink(near_out, far_out, low)):
        weight = part[:, depth : depth + 1].astype(F32)
        cotangent.append((weight * (weight * rows) * scale).astype(BF))
    c_near, c_far = grow(cotangent, low)

    g_near = gates_of(c_near, student_down, ab_near)
    c_far, g_near = lax.optimization_barrier((c_far, g_near))
    side, cs = core.astype(jnp.int32).reshape(1), c_near + c_far
    *send, g_far = send_half(side, cs, xt, student_down, g_near, ht, ab_far)
    tall_got, low_got = (lax.ppermute(v, "dp", [(0, 1), (1, 0)]) for v in send)
    tall, low_kept = keep_half(side, cs, xt, g_near, g_far, ht)
    tall, low_kept = tall + tall_got.astype(F32), low_kept + low_got.astype(F32)
    return tall[:, 0:128], tall[:, 128:256], low_kept


def solution(mesh):
    placed = (
        P(("dp", "expert"), None),
        P(("dp", "expert")),
        P(("dp", "expert"), None),
        P(),
        P(None, "expert"),
        P(None, "expert"),
        P("expert", None),
        P(None, "expert"),
        P(None, "expert"),
        P("expert", None),
    )
    return jax.shard_map(
        per_device,
        mesh=mesh,
        in_specs=placed,
        out_specs=(P("dp", "expert"), P("dp", "expert"), P("expert", "dp")),
        check_vma=False,
    )
```

```python
import functools
import math

import jax
import jax.numpy as jnp
from jax import lax
from jax.experimental import pallas as pl
from jax.experimental.pallas import tpu as pltpu
from jax.sharding import PartitionSpec as P

F = 4096
E_ORIG = 4
META = 128
BLOCK = 1280
BF = jnp.bfloat16
F32 = jnp.float32
AXES = ("dp", "expert")
SIDE = 4


def coords(device):
    return device // 64, {"z": (device // 16) % SIDE, "y": (device // 4) % SIDE, "x": device % SIDE}


def number(core, at):
    return core * 64 + at["z"] * 16 + at["y"] * 4 + at["x"]


def join(*parts):
    return jnp.concatenate(parts, axis=0)


ORDERS = (("x", "y", "z"), ("z", "x", "y"), ("y", "z", "x"))
PIECES = range(3)
CROSS = (3, 5)


def step_pairs(piece, step):
    axis, pairs = ORDERS[piece][step // 2], []
    for device in range(128):
        core, at = coords(device)
        bits = (1, 3)[(step + core) % 2]
        pairs.append((device, number(core ^ (step in CROSS), {**at, axis: at[axis] ^ bits})))
    return pairs


def hop(value, piece, step):
    return lax.ppermute(value, AXES, step_pairs(piece, step))


def hop_back(value, piece, step):
    return lax.ppermute(value, AXES, [(to, own) for own, to in step_pairs(piece, step)])


def add(mine, got):
    return mine.astype(F32) + got.astype(F32)


def grow(parts):
    for step in (2, 3, 4):
        parts = [join(v, hop(v, p, step)) for p, v in enumerate(parts)]
    return parts[::-1], [hop(v, p, 5) for p, v in enumerate(parts)][::-1]


def shrink(near, far, beside):
    sums = []
    for p in PIECES:
        mine, theirs = near[2 - p], far[2 - p]
        for step in (5, 4, 3, 2):
            got = hop_back(theirs.astype(BF), p, step)
            if step == 2:
                mine = add(mine, got)
                continue
            half = mine.shape[0] // 2
            theirs, mine = add(mine[half:], got[half:]), add(mine[:half], got[:half])
            if (p, step) == (0, 5):
                theirs, beside = lax.optimization_barrier((theirs.astype(BF), beside))
        sums.append(mine)
    for step in (1, 0):
        sums = [add(v, hop(v.astype(BF), p, step)) for p, v in enumerate(sums)]
    return sums, beside


def line_up_kernel(place_ref, mine, got, out):
    row = lax.broadcasted_iota(jnp.int32, (16, 32), 0)
    column = lax.broadcasted_iota(jnp.int32, (16, 32), 1)
    block, token = column // 8, column % 8
    place = jnp.zeros((16, 32), jnp.int32)
    for i in range(SIDE):
        place = jnp.where(block == i, place_ref[i], place)
    pick = jnp.where((row == place * 4 + token) & (token < 4), 1.0, 0.0).astype(BF)
    rows = jnp.concatenate([mine[...], got[...]], axis=0)
    out[...] = jnp.dot(pick, rows, preferred_element_type=F32).astype(BF)


def line_up(places, mine, got):
    vmem = pl.BlockSpec(memory_space=pltpu.VMEM)
    return pl.pallas_call(
        line_up_kernel,
        out_shape=jax.ShapeDtypeStruct((16, mine.shape[1]), BF),
        in_specs=[pl.BlockSpec(memory_space=pltpu.SMEM), vmem, vmem],
        out_specs=vmem,
        compiler_params=pltpu.CompilerParams(vmem_limit_bytes=16 << 20),
    )(places, mine, got)


def pack_kernel(tokens, weight, ids, *outs):
    rows = tokens.shape[0]
    row = lax.broadcasted_iota(jnp.int32, (rows, rows), 0)
    diagonal = row == lax.broadcasted_iota(jnp.int32, (rows, rows), 1)
    column = lambda v: jnp.sum(jnp.where(diagonal, v.astype(F32), 0.0), axis=1, keepdims=True)
    place = lax.broadcasted_iota(jnp.int32, (rows, META), 1)
    meta = jnp.where(place == 0, column(weight[...]), jnp.where(place == 1, column(ids[...]), 0.0))
    both = jnp.concatenate([tokens[...].astype(F32), meta], axis=1)
    empty = jnp.zeros((4, both.shape[1]), F32)
    for i, out in enumerate(outs):
        out[...] = jnp.concatenate([both[4 * i : 4 * i + 4], empty], axis=0).astype(BF)


def pack(tokens, weight, ids):
    whole = lambda *shape: pl.BlockSpec(shape, lambda n: (0, 0))
    rows, width = tokens.shape
    return pl.pallas_call(
        pack_kernel,
        grid=(1,),
        out_shape=[jax.ShapeDtypeStruct((8, width + META), BF)] * 3,
        in_specs=[whole(rows, width), whole(1, rows), whole(1, rows)],
        out_specs=[whole(8, width + META)] * 3,
        compiler_params=pltpu.CompilerParams(vmem_limit_bytes=60 << 20),
    )(tokens, weight.reshape(1, -1), ids.reshape(1, -1))


def first_gather(blocks, core, at):
    flips = jnp.where(core == 0, jnp.array([0, 1, 3, 2]), jnp.array([0, 3, 1, 2])).astype(jnp.int32)
    parts = []
    for p, mine in enumerate(blocks):
        mine = join(mine, hop(mine, p, 0))
        parts.append(line_up(at[ORDERS[p][0]] ^ flips, mine, hop(mine, p, 1)))
    return parts


VMEM = pl.BlockSpec(memory_space=pltpu.VMEM)
SMEM = pl.BlockSpec(memory_space=pltpu.SMEM)
PARAMS = pltpu.CompilerParams(vmem_limit_bytes=16 << 20)


def shaped(*shape, dtype=BF):
    return jax.ShapeDtypeStruct(shape, dtype)


def dot(a, b):
    return jnp.dot(a, b, preferred_element_type=F32)


def forward_kernel(count, info, *refs):
    xs, (tg, tu, sg, su, sd, td) = refs[:count], refs[count : count + 6]
    outs, (h_ref, ab_ref, hidden) = refs[count + 6 : 2 * count + 6], refs[2 * count + 6 :]
    depth = tg.shape[0]
    for i, x_ref in enumerate(xs):
        rows = slice(128 * i, 128 * (i + 1))
        x = x_ref[:, 0:depth]
        ids = x_ref[:, depth : depth + META].astype(F32)[:, 1:2]
        mask_t = ids == info[0].astype(F32)
        mask_s = jnp.zeros(ids.shape, F32)
        for e in range(E_ORIG):
            mask_s = mask_s + jnp.where(ids == float(e), info[1 + e].astype(F32), 0.0)
        mask_s = mask_s > 0.5
        both = dot(x, jnp.concatenate([sg[...], su[...]], axis=1))
        gate, up = both[:, 0:128], both[:, 128:256]
        sig = jax.nn.sigmoid(gate)
        silu = gate * sig
        hid_s = jnp.where(mask_s, silu * up, 0.0)
        hidden[rows, 0:128] = hid_s.astype(BF)
        ab_ref[rows, 0:128] = jnp.where(mask_s, up * sig * (1.0 + gate * (1.0 - sig)), 0.0)
        ab_ref[rows, 128:256] = jnp.where(mask_s, silu, 0.0)
        gate, up = dot(x, tg[...]), dot(x, tu[...])
        hid_t = gate * jax.nn.sigmoid(gate) * up
        hidden[rows, 128:384] = jnp.where(mask_t, -hid_t, 0.0).astype(BF)
    for i, out in enumerate(outs):
        h = hidden[128 * i : 128 * (i + 1), :]
        for at in range(0, depth, BLOCK):
            n = slice(at, at + BLOCK)
            out[:, n] = dot(h, jnp.concatenate([sd[:, n], td[:, n]], axis=0)).astype(BF)
        h_ref[128 * i : 128 * (i + 1), :] = h[:, 0:128]


def forward(info, chunks, *weights):
    count, depth = len(chunks), weights[0].shape[0]
    rows = 128 * count
    *outs, h, ab = pl.pallas_call(
        functools.partial(forward_kernel, count),
        out_shape=[shaped(128, depth)] * count + [shaped(rows, 128), shaped(rows, 256, dtype=F32)],
        in_specs=[SMEM] + [VMEM] * (count + 6),
        out_specs=[VMEM] * (count + 2),
        scratch_shapes=[pltpu.VMEM((rows, 384), BF)],
        compiler_params=PARAMS,
        cost_estimate=pl.CostEstimate(flops=2 * rows * depth * 1152, bytes_accessed=2 * depth * (rows + 1152), transcendentals=0),
    )(info, *chunks, *weights)
    return outs, h, ab


def dgates(c, sd, ab):
    dhidden = lax.dot_general(c, sd, (((1,), (1,)), ((), ())), preferred_element_type=F32)
    return jnp.concatenate([dhidden * ab[:, 0:128], dhidden * ab[:, 128:256]], axis=1).astype(BF)


def dgates_kernel(*refs):
    cs, (sd, ab, g) = refs[:-3], refs[-3:]
    for i, c in enumerate(cs):
        rows = slice(128 * i, 128 * (i + 1))
        g[rows, :] = dgates(c[...], sd[...], ab[rows, :])


def gates_of(cs, sd, ab):
    rows = 128 * len(cs)
    return pl.pallas_call(
        dgates_kernel,
        out_shape=shaped(rows, 256),
        in_specs=[VMEM] * (len(cs) + 2),
        out_specs=VMEM,
        compiler_params=PARAMS,
        cost_estimate=pl.CostEstimate(flops=2 * rows * sd.size, bytes_accessed=2 * rows * sd.shape[1], transcendentals=0),
    )(*cs, sd, ab)


def turn_kernel(*refs):
    xs, (h1, h2, out, ht) = refs[:-4], refs[-4:]
    for i, r in enumerate(xs):
        out[:, 128 * i : 128 * (i + 1)] = r[...].T

    @pl.when(pl.program_id(0) == 0)
    def _():
        ht[...] = jnp.concatenate([h1[...].T, h2[...].T], axis=1)


def turn(xs, h1, h2, width):
    rows = 128 * len(xs)
    whole = lambda *shape: pl.BlockSpec(shape, lambda n: (0, 0))
    return pl.pallas_call(
        turn_kernel,
        grid=(width // BLOCK,),
        out_shape=[shaped(width, rows), shaped(128, rows)],
        in_specs=[pl.BlockSpec((128, BLOCK), lambda n: (0, n))] * len(xs) + [whole(rows // 2, 128)] * 2,
        out_specs=[pl.BlockSpec((BLOCK, rows), lambda n: (n, 0)), whole(128, rows)],
        compiler_params=PARAMS,
        cost_estimate=pl.CostEstimate(flops=0, bytes_accessed=4 * rows * width, transcendentals=0),
    )(*xs, h1, h2)


def tall_half(side, xt, g, tall):
    for at in range(0, tall.shape[0], BLOCK):
        here = pl.ds(pl.multiple_of(side * tall.shape[0] + at, 128), BLOCK)
        tall[at : at + BLOCK, :] = dot(xt[here, :], g).astype(tall.dtype)


def low_half(side, cs, ht, low):
    for at in range(0, low.shape[1], BLOCK):
        here = pl.ds(pl.multiple_of(side * low.shape[1] + at, 128), BLOCK)
        total = None
        for i in range(0, len(cs), 2):
            c = jnp.concatenate([r[:, here] for r in cs[i : i + 2]], axis=0)
            part = dot(ht[:, 128 * i : 128 * (i + 2)], c)
            total = part if total is None else total + part
        low[:, at : at + BLOCK] = total.astype(low.dtype)


def together(refs):
    return jnp.concatenate([r[...] for r in refs], axis=0)


def send_tall_kernel(core, c, xt, sd, ab, *refs):
    gs, tall, g_last = refs[:-2], refs[-2], refs[-1]
    g_last[...] = dgates(c[...], sd[...], ab)
    tall_half(1 - core[0], xt, together((*gs, g_last)), tall)


def send_tall(core, c, xt, sd, ab, gs):
    width = sd.shape[1]
    return pl.pallas_call(
        send_tall_kernel,
        out_shape=[shaped(width // 2, 256), shaped(128, 256)],
        in_specs=[SMEM] + [VMEM] * (4 + len(gs)),
        out_specs=[VMEM] * 2,
        compiler_params=PARAMS,
        cost_estimate=pl.CostEstimate(flops=768 * width * 256, bytes_accessed=768 * width, transcendentals=0),
    )(core, c, xt, sd, ab, *gs)


def send_low_kernel(core, ht, *refs):
    low_half(1 - core[0], refs[:-1], ht, refs[-1])


def send_low(core, ht, cs):
    width = cs[0].shape[1]
    return pl.pallas_call(
        send_low_kernel,
        out_shape=shaped(128, width // 2),
        in_specs=[SMEM] + [VMEM] * (1 + len(cs)),
        out_specs=VMEM,
        compiler_params=PARAMS,
        cost_estimate=pl.CostEstimate(flops=768 * width * 128, bytes_accessed=768 * width, transcendentals=0),
    )(core, ht, *cs)


def keep_kernel(core, xt, ht, *refs):
    cs, gs, (tall, low) = refs[0:6], refs[6:-2], refs[-2:]
    tall_half(core[0], xt, together(gs), tall)
    low_half(core[0], cs, ht, low)


def keep_half(core, xt, ht, cs, gs):
    width = cs[0].shape[1] // 2
    return pl.pallas_call(
        keep_kernel,
        out_shape=[shaped(width, 256, dtype=F32), shaped(128, width, dtype=F32)],
        in_specs=[SMEM] + [VMEM] * (8 + len(gs)),
        out_specs=[VMEM] * 2,
        compiler_params=PARAMS,
        cost_estimate=pl.CostEstimate(flops=768 * width * 768, bytes_accessed=4 * 768 * width, transcendentals=0),
    )(core, xt, ht, *cs, *gs)


def per_device(
    tokens,
    router_weight,
    initial_id,
    group_map,
    teacher_gate,
    teacher_up,
    teacher_down,
    student_gate,
    student_up,
    student_down,
):
    core, owner = lax.axis_index("dp"), lax.axis_index("expert")
    total = tokens.shape[0] * 128
    at = {"z": owner // 16, "y": (owner // SIDE) % SIDE, "x": owner % SIDE}
    teacher_expert = owner * teacher_gate.shape[1] // F
    student_expert = owner * student_gate.shape[1] // F
    info = jnp.concatenate([teacher_expert.astype(jnp.int32).reshape(1), (group_map == student_expert).astype(jnp.int32)])

    parts = first_gather(pack(tokens, router_weight, initial_id), core, at)
    near, far = grow(parts)

    weights = (teacher_gate, teacher_up, student_gate, student_up, student_down, teacher_down)
    near_out, h_near, ab_near = forward(info, near, *weights)
    far, h_near = lax.optimization_barrier((far, h_near))
    far_out, h_far, ab_far = forward(info, far, *weights)

    depth, scale = tokens.shape[1], 1.0 / math.sqrt(total)
    sums, (xt, ht) = shrink(near_out, far_out, turn(near + far, h_near, h_far, depth))
    cotangent = []
    for part, rows in zip(parts, sums):
        weight = part[:, depth : depth + 1].astype(F32)
        cotangent.append((weight * (weight * rows) * scale).astype(BF))
    c_near, c_far = grow(cotangent)

    abs_far = [ab_far[128 * i : 128 * (i + 1)] for i in PIECES]
    gs = [gates_of(c_near, student_down, ab_near)]
    gs += [gates_of([c], student_down, ab) for c, ab in zip(c_far[:2], abs_far)]
    last, gs = lax.optimization_barrier((c_far[2], gs))
    side, cs = core.astype(jnp.int32).reshape(1), [*c_near, *c_far[:2], last]
    tall_sent, g_last = send_tall(side, last, xt, student_down, abs_far[2], gs)
    low_sent = send_low(side, ht, cs)
    tall_got, low_got = (lax.ppermute(v, "dp", [(0, 1), (1, 0)]) for v in (tall_sent, low_sent))
    tall, low = keep_half(side, xt, ht, cs, [*gs, g_last])
    tall, low = tall + tall_got.astype(F32), low + low_got.astype(F32)
    return tall[:, 0:128], tall[:, 128:256], low


def solution(mesh):
    placed = (
        P(("dp", "expert"), None),
        P(("dp", "expert")),
        P(("dp", "expert"), None),
        P(),
        P(None, "expert"),
        P(None, "expert"),
        P("expert", None),
        P(None, "expert"),
        P(None, "expert"),
        P("expert", None),
    )
    return jax.shard_map(
        per_device,
        mesh=mesh,
        in_specs=placed,
        out_specs=(P("dp", "expert"), P("dp", "expert"), P("expert", "dp")),
        check_vma=False,
    )
```

```python
import functools
import math

import jax
import jax.numpy as jnp
from jax import lax
from jax.experimental import pallas as pl
from jax.experimental.pallas import tpu as pltpu
from jax.sharding import PartitionSpec as P

F = 4096
E_ORIG = 4
META = 128
BLOCK = 1280
BF = jnp.bfloat16
F32 = jnp.float32
AXES = ("dp", "expert")
SIDE = 4


def coords(device):
    return device // 64, {"z": (device // 16) % SIDE, "y": (device // 4) % SIDE, "x": device % SIDE}


def number(core, at):
    return core * 64 + at["z"] * 16 + at["y"] * 4 + at["x"]


def join(*parts):
    return jnp.concatenate(parts, axis=0)


ORDERS = (("x", "y", "z"), ("z", "x", "y"), ("y", "z", "x"))
PIECES = range(3)
CROSS = (3, 5)


def step_pairs(piece, step):
    axis, pairs = ORDERS[piece][step // 2], []
    for device in range(128):
        core, at = coords(device)
        bits = (1, 3)[(step + core) % 2]
        pairs.append((device, number(core ^ (step in CROSS), {**at, axis: at[axis] ^ bits})))
    return pairs


def hop(value, piece, step):
    return lax.ppermute(value, AXES, step_pairs(piece, step))


def hop_back(value, piece, step):
    return lax.ppermute(value, AXES, [(to, own) for own, to in step_pairs(piece, step)])


def add(mine, got):
    return mine.astype(F32) + got.astype(F32)


def grow(parts):
    for step in (2, 3, 4):
        parts = [join(v, hop(v, p, step)) for p, v in enumerate(parts)]
    return parts[::-1], [hop(v, p, 5) for p, v in enumerate(parts)][::-1]


def shrink(near, far, beside):
    sums = []
    for p in PIECES:
        mine, theirs = near[2 - p], far[2 - p]
        for step in (5, 4, 3, 2):
            got = hop_back(theirs.astype(BF), p, step)
            if step == 2:
                mine = add(mine, got)
                continue
            half = mine.shape[0] // 2
            theirs, mine = add(mine[half:], got[half:]), add(mine[:half], got[:half])
            if (p, step) == (0, 5):
                theirs, beside = lax.optimization_barrier((theirs.astype(BF), beside))
        sums.append(mine)
    for step in (1, 0):
        sums = [add(v, hop(v.astype(BF), p, step)) for p, v in enumerate(sums)]
    return sums, beside


def line_up_kernel(place_ref, mine, got, out):
    row = lax.broadcasted_iota(jnp.int32, (16, 32), 0)
    column = lax.broadcasted_iota(jnp.int32, (16, 32), 1)
    block, token = column // 8, column % 8
    place = jnp.zeros((16, 32), jnp.int32)
    for i in range(SIDE):
        place = jnp.where(block == i, place_ref[i], place)
    pick = jnp.where((row == place * 4 + token) & (token < 4), 1.0, 0.0).astype(BF)
    rows = jnp.concatenate([mine[...], got[...]], axis=0)
    out[...] = jnp.dot(pick, rows, preferred_element_type=F32).astype(BF)


def line_up(places, mine, got):
    vmem = pl.BlockSpec(memory_space=pltpu.VMEM)
    return pl.pallas_call(
        line_up_kernel,
        out_shape=jax.ShapeDtypeStruct((16, mine.shape[1]), BF),
        in_specs=[pl.BlockSpec(memory_space=pltpu.SMEM), vmem, vmem],
        out_specs=vmem,
        compiler_params=pltpu.CompilerParams(vmem_limit_bytes=16 << 20),
    )(places, mine, got)


def pack_kernel(tokens, weight, ids, *outs):
    rows = tokens.shape[0]
    row = lax.broadcasted_iota(jnp.int32, (rows, rows), 0)
    diagonal = row == lax.broadcasted_iota(jnp.int32, (rows, rows), 1)
    column = lambda v: jnp.sum(jnp.where(diagonal, v.astype(F32), 0.0), axis=1, keepdims=True)
    place = lax.broadcasted_iota(jnp.int32, (rows, META), 1)
    meta = jnp.where(place == 0, column(weight[...]), jnp.where(place == 1, column(ids[...]), 0.0))
    both = jnp.concatenate([tokens[...].astype(F32), meta], axis=1)
    empty = jnp.zeros((4, both.shape[1]), F32)
    for i, out in enumerate(outs):
        out[...] = jnp.concatenate([both[4 * i : 4 * i + 4], empty], axis=0).astype(BF)


def pack(tokens, weight, ids):
    whole = lambda *shape: pl.BlockSpec(shape, lambda n: (0, 0))
    rows, width = tokens.shape
    return pl.pallas_call(
        pack_kernel,
        grid=(1,),
        out_shape=[jax.ShapeDtypeStruct((8, width + META), BF)] * 3,
        in_specs=[whole(rows, width), whole(1, rows), whole(1, rows)],
        out_specs=[whole(8, width + META)] * 3,
        compiler_params=pltpu.CompilerParams(vmem_limit_bytes=60 << 20),
    )(tokens, weight.reshape(1, -1), ids.reshape(1, -1))


def first_gather(blocks, core, at):
    flips = jnp.where(core == 0, jnp.array([0, 1, 3, 2]), jnp.array([0, 3, 1, 2])).astype(jnp.int32)
    parts = []
    for p, mine in enumerate(blocks):
        mine = join(mine, hop(mine, p, 0))
        parts.append(line_up(at[ORDERS[p][0]] ^ flips, mine, hop(mine, p, 1)))
    return parts


VMEM = pl.BlockSpec(memory_space=pltpu.VMEM)
SMEM = pl.BlockSpec(memory_space=pltpu.SMEM)
PARAMS = pltpu.CompilerParams(vmem_limit_bytes=16 << 20)


def shaped(*shape, dtype=BF):
    return jax.ShapeDtypeStruct(shape, dtype)


def dot(a, b):
    return jnp.dot(a, b, preferred_element_type=F32)


def forward_kernel(count, info, *refs):
    xs, (tg, tu, sg, su, sd, td) = refs[:count], refs[count : count + 6]
    outs, (h_ref, ab_ref, hidden) = refs[count + 6 : 2 * count + 6], refs[2 * count + 6 :]
    depth = tg.shape[0]
    for i, x_ref in enumerate(xs):
        rows = slice(128 * i, 128 * (i + 1))
        x = x_ref[:, 0:depth]
        ids = x_ref[:, depth : depth + META].astype(F32)[:, 1:2]
        mask_t = ids == info[0].astype(F32)
        mask_s = jnp.zeros(ids.shape, F32)
        for e in range(E_ORIG):
            mask_s = mask_s + jnp.where(ids == float(e), info[1 + e].astype(F32), 0.0)
        mask_s = mask_s > 0.5
        both = dot(x, jnp.concatenate([sg[...], su[...]], axis=1))
        gate, up = both[:, 0:128], both[:, 128:256]
        sig = jax.nn.sigmoid(gate)
        silu = gate * sig
        hid_s = jnp.where(mask_s, silu * up, 0.0)
        hidden[rows, 0:128] = hid_s.astype(BF)
        ab_ref[rows, 0:128] = jnp.where(mask_s, up * sig * (1.0 + gate * (1.0 - sig)), 0.0)
        ab_ref[rows, 128:256] = jnp.where(mask_s, silu, 0.0)
        gate, up = dot(x, tg[...]), dot(x, tu[...])
        hid_t = gate * jax.nn.sigmoid(gate) * up
        hidden[rows, 128:384] = jnp.where(mask_t, -hid_t, 0.0).astype(BF)
    for i, out in enumerate(outs):
        h = hidden[128 * i : 128 * (i + 1), :]
        for at in range(0, depth, BLOCK):
            n = slice(at, at + BLOCK)
            out[:, n] = dot(h, jnp.concatenate([sd[:, n], td[:, n]], axis=0)).astype(BF)
        h_ref[128 * i : 128 * (i + 1), :] = h[:, 0:128]


def forward(info, chunks, *weights):
    count, depth = len(chunks), weights[0].shape[0]
    rows = 128 * count
    *outs, h, ab = pl.pallas_call(
        functools.partial(forward_kernel, count),
        out_shape=[shaped(128, depth)] * count + [shaped(rows, 128), shaped(rows, 256, dtype=F32)],
        in_specs=[SMEM] + [VMEM] * (count + 6),
        out_specs=[VMEM] * (count + 2),
        scratch_shapes=[pltpu.VMEM((rows, 384), BF)],
        compiler_params=PARAMS,
        cost_estimate=pl.CostEstimate(flops=2 * rows * depth * 1152, bytes_accessed=2 * depth * (rows + 1152), transcendentals=0),
    )(info, *chunks, *weights)
    return outs, h, ab


def dgates(c, sd, ab):
    dhidden = lax.dot_general(c, sd, (((1,), (1,)), ((), ())), preferred_element_type=F32)
    return jnp.concatenate([dhidden * ab[:, 0:128], dhidden * ab[:, 128:256]], axis=1).astype(BF)


def dgates_kernel(*refs):
    cs, (sd, ab, g) = refs[:-3], refs[-3:]
    for i, c in enumerate(cs):
        rows = slice(128 * i, 128 * (i + 1))
        g[rows, :] = dgates(c[...], sd[...], ab[rows, :])


def gates_of(cs, sd, ab):
    rows = 128 * len(cs)
    return pl.pallas_call(
        dgates_kernel,
        out_shape=shaped(rows, 256),
        in_specs=[VMEM] * (len(cs) + 2),
        out_specs=VMEM,
        compiler_params=PARAMS,
        cost_estimate=pl.CostEstimate(flops=2 * rows * sd.size, bytes_accessed=2 * rows * sd.shape[1], transcendentals=0),
    )(*cs, sd, ab)


def turn_kernel(*refs):
    xs, (h1, h2, out, ht) = refs[:-4], refs[-4:]
    for i, r in enumerate(xs):
        out[:, 128 * i : 128 * (i + 1)] = r[...].T

    @pl.when(pl.program_id(0) == 0)
    def _():
        ht[...] = jnp.concatenate([h1[...].T, h2[...].T], axis=1)


def turn(xs, h1, h2, width):
    rows = 128 * len(xs)
    whole = lambda *shape: pl.BlockSpec(shape, lambda n: (0, 0))
    return pl.pallas_call(
        turn_kernel,
        grid=(width // BLOCK,),
        out_shape=[shaped(width, rows), shaped(128, rows)],
        in_specs=[pl.BlockSpec((128, BLOCK), lambda n: (0, n))] * len(xs) + [whole(rows // 2, 128)] * 2,
        out_specs=[pl.BlockSpec((BLOCK, rows), lambda n: (n, 0)), whole(128, rows)],
        compiler_params=PARAMS,
        cost_estimate=pl.CostEstimate(flops=0, bytes_accessed=4 * rows * width, transcendentals=0),
    )(*xs, h1, h2)


def tall_half(side, xt, g, tall):
    for at in range(0, tall.shape[0], BLOCK):
        here = pl.ds(pl.multiple_of(side * tall.shape[0] + at, 128), BLOCK)
        tall[at : at + BLOCK, :] = dot(xt[here, :], g).astype(tall.dtype)


def low_half(side, cs, ht, low):
    for at in range(0, low.shape[1], BLOCK):
        here = pl.ds(pl.multiple_of(side * low.shape[1] + at, 128), BLOCK)
        total = None
        for i in range(0, len(cs), 2):
            c = jnp.concatenate([r[:, here] for r in cs[i : i + 2]], axis=0)
            part = dot(ht[:, 128 * i : 128 * (i + 2)], c)
            total = part if total is None else total + part
        low[:, at : at + BLOCK] = total.astype(low.dtype)


def together(refs):
    return jnp.concatenate([r[...] for r in refs], axis=0)


def send_tall_kernel(core, c, xt, sd, ab, *refs):
    gs, tall, g_last = refs[:-2], refs[-2], refs[-1]
    g_last[...] = dgates(c[...], sd[...], ab)
    tall_half(1 - core[0], xt, together((*gs, g_last)), tall)


def send_tall(core, c, xt, sd, ab, gs):
    width = sd.shape[1]
    return pl.pallas_call(
        send_tall_kernel,
        out_shape=[shaped(width // 2, 256), shaped(128, 256)],
        in_specs=[SMEM] + [VMEM] * (4 + len(gs)),
        out_specs=[VMEM] * 2,
        compiler_params=PARAMS,
        cost_estimate=pl.CostEstimate(flops=768 * width * 256, bytes_accessed=768 * width, transcendentals=0),
    )(core, c, xt, sd, ab, *gs)


def send_low_kernel(core, ht, *refs):
    low_half(1 - core[0], refs[:-1], ht, refs[-1])


def send_low(core, ht, cs):
    width = cs[0].shape[1]
    return pl.pallas_call(
        send_low_kernel,
        out_shape=shaped(128, width // 2),
        in_specs=[SMEM] + [VMEM] * (1 + len(cs)),
        out_specs=VMEM,
        compiler_params=PARAMS,
        cost_estimate=pl.CostEstimate(flops=768 * width * 128, bytes_accessed=768 * width, transcendentals=0),
    )(core, ht, *cs)


def keep_tall_kernel(core, xt, *refs):
    tall_half(core[0], xt, together(refs[:-1]), refs[-1])


def keep_tall(core, xt, gs):
    width = xt.shape[0]
    return pl.pallas_call(
        keep_tall_kernel,
        out_shape=shaped(width // 2, 256, dtype=F32),
        in_specs=[SMEM] + [VMEM] * (1 + len(gs)),
        out_specs=VMEM,
        compiler_params=PARAMS,
        cost_estimate=pl.CostEstimate(flops=768 * width * 256, bytes_accessed=768 * width, transcendentals=0),
    )(core, xt, *gs)


def keep_low_kernel(core, ht, got, *refs):
    low_half(core[0], refs[:-1], ht, refs[-1])
    refs[-1][...] += got[...].astype(F32)


def keep_low(core, ht, got, cs):
    width = cs[0].shape[1]
    return pl.pallas_call(
        keep_low_kernel,
        out_shape=shaped(128, width // 2, dtype=F32),
        in_specs=[SMEM] + [VMEM] * (2 + len(cs)),
        out_specs=VMEM,
        compiler_params=PARAMS,
        cost_estimate=pl.CostEstimate(flops=768 * width * 128, bytes_accessed=768 * width, transcendentals=0),
    )(core, ht, got, *cs)


def per_device(
    tokens,
    router_weight,
    initial_id,
    group_map,
    teacher_gate,
    teacher_up,
    teacher_down,
    student_gate,
    student_up,
    student_down,
):
    core, owner = lax.axis_index("dp"), lax.axis_index("expert")
    total = tokens.shape[0] * 128
    at = {"z": owner // 16, "y": (owner // SIDE) % SIDE, "x": owner % SIDE}
    teacher_expert = owner * teacher_gate.shape[1] // F
    student_expert = owner * student_gate.shape[1] // F
    info = jnp.concatenate([teacher_expert.astype(jnp.int32).reshape(1), (group_map == student_expert).astype(jnp.int32)])

    parts = first_gather(pack(tokens, router_weight, initial_id), core, at)
    near, far = grow(parts)

    weights = (teacher_gate, teacher_up, student_gate, student_up, student_down, teacher_down)
    near_out, h_near, ab_near = forward(info, near, *weights)
    far, h_near = lax.optimization_barrier((far, h_near))
    far_out, h_far, ab_far = forward(info, far, *weights)

    depth, scale = tokens.shape[1], 1.0 / math.sqrt(total)
    sums, (xt, ht) = shrink(near_out, far_out, turn(near + far, h_near, h_far, depth))
    cotangent = []
    for part, rows in zip(parts, sums):
        weight = part[:, depth : depth + 1].astype(F32)
        cotangent.append((weight * (weight * rows) * scale).astype(BF))
    c_near, c_far = grow(cotangent)

    abs_far = [ab_far[128 * i : 128 * (i + 1)] for i in PIECES]
    gs = [gates_of(c_near, student_down, ab_near)]
    gs += [gates_of([c], student_down, ab) for c, ab in zip(c_far[:2], abs_far)]
    last, gs = lax.optimization_barrier((c_far[2], gs))
    side, cs = core.astype(jnp.int32).reshape(1), [*c_near, *c_far[:2], last]
    tall_sent, g_last = send_tall(side, last, xt, student_down, abs_far[2], gs)
    low_sent = send_low(side, ht, cs)
    tall_got, low_got = (lax.ppermute(v, "dp", [(0, 1), (1, 0)]) for v in (tall_sent, low_sent))
    tall = keep_tall(side, xt, [*gs, g_last]) + tall_got.astype(F32)
    low = keep_low(side, ht, low_got, cs)
    return tall[:, 0:128], tall[:, 128:256], low


def solution(mesh):
    placed = (
        P(("dp", "expert"), None),
        P(("dp", "expert")),
        P(("dp", "expert"), None),
        P(),
        P(None, "expert"),
        P(None, "expert"),
        P("expert", None),
        P(None, "expert"),
        P(None, "expert"),
        P("expert", None),
    )
    return jax.shard_map(
        per_device,
        mesh=mesh,
        in_specs=placed,
        out_specs=(P("dp", "expert"), P("dp", "expert"), P("expert", "dp")),
        check_vma=False,
    )
```
